32 devices in a mesh: row: 8 (over z, x), col: 4 (over y, core).
Axes of the slice: x: 2, y: 2, z: 4, core: 2. Of those that a mesh axis runs over, the one named last changes fastest.
Arguments:
- rhs: float32 [32, 64, 128], P(('row', 'col')), may hold values from -16 to 16
- item_factors: bfloat16 [256, 64, 128], P('col'), may hold values from -0.125 to 0.125
- slot_users: int32 [8, 4, 96], P('row', 'col'), may hold values from 0 to 3, as said below
- slot_items: int32 [8, 4, 96], P('row', 'col'), may hold values from 0 to 63
- slot_counts: int32 [8, 4], P('row', 'col'), may hold values from 12 to 96, as said below
- mask_words: int32 [8, 4, 96, 16, 128], P('row', 'col'), may hold values from 0 to 255
- self_tiles: int32 [32, 128, 128], P(('row', 'col')), may hold values from 0 to 3, as said below
- next_tiles: int32 [32, 128, 128], P(('row', 'col')), may hold values from 0 to 3, as said below
Outputs:
- solution: float32 [32, 64, 128], P(('row', 'col'))
- residual: float32 [32, 64, 128], P(('row', 'col'))
The draws below stay inside these ranges and needn't reach their ends.
Inputs may be any that keep to these rules, and one draw needn't show every extreme that they name: `slot_users`: on each grid cell the 96 slots name distinct pairs of user block and item block. Some grid cells use all 96 slots; slots at positions slot_counts or later are ignored. `self_tiles`: most weights are zero. `next_tiles`: most weights are zero.
All inputs are finite; a program needn't handle non-finite values.
Results may differ from the reference program's by a relative error of at most 0.018.
Values may be sent and summed in bfloat16 or wider, within the bound.
No kernel may reach another device: no remote copies, remote signals or barrier semaphores. Data moves between devices by JAX's collectives and lax.ppermute only.
A program may use at most 64 MiB of HBM per device.

```python
import jax
import jax.numpy as jnp
from jax import lax

BLOCK = 128
K = 64
ITERS = 2
UB_DEV = 1
IBC = 64
S_CAP = 96
GRID_ROWS = 8
GRID_COLS = 4
ROW_BLOCKS = 4
USER_BLOCKS = 32
USERS = 4096
ITEM_BLOCKS = 256


def draw_rhs(key, part):
    position = (jnp.arange(USER_BLOCKS, dtype=jnp.float32)[:, None, None] * BLOCK + jnp.arange(BLOCK, dtype=jnp.float32)[None, None, :]) / USERS
    base = jnp.clip(jax.random.normal(key, (USER_BLOCKS, K, BLOCK), jnp.float32), -5.0, 5.0)
    return base * jnp.power(3.0, position)


def slot_table(key):
    inner = jax.random.fold_in(key, 11)
    keys = jax.random.split(inner, GRID_ROWS * GRID_COLS)
    table = jax.vmap(lambda single: jax.random.permutation(single, ROW_BLOCKS * IBC))(keys)
    return table[:, :S_CAP].reshape(GRID_ROWS, GRID_COLS, S_CAP).astype(jnp.int32)


def draw_slot_users(key, part):
    return slot_table(key) // IBC


def draw_slot_items(key, part):
    return slot_table(key) % IBC


def draw_slot_counts(key, part):
    first, second, third = jax.random.split(jax.random.fold_in(key, 5), 3)
    light = jax.random.randint(first, (GRID_ROWS, GRID_COLS), S_CAP // 8, S_CAP // 2 + 1)
    heavy = jax.random.randint(second, (GRID_ROWS, GRID_COLS), 0, 8) == 0
    chosen = jax.random.randint(third, (), 0, GRID_ROWS * GRID_COLS)
    forced = jnp.arange(GRID_ROWS * GRID_COLS).reshape(GRID_ROWS, GRID_COLS) == chosen
    return jnp.where(heavy | forced, S_CAP, light).astype(jnp.int32)


def sparse_weights(key):
    values = jax.random.randint(key, (USER_BLOCKS, BLOCK, BLOCK), 0, 32)
    return jnp.maximum(values - 28, 0).astype(jnp.int32)


def draw_self_tiles(key, part):
    return sparse_weights(jax.random.fold_in(key, 21))


def draw_next_tiles(key, part):
    return sparse_weights(jax.random.fold_in(key, 31))


def plant(values, rng, low, largest):
    extent = values.shape
    spot = [jax.random.randint(jax.random.fold_in(rng, axis), (), 0, extent[axis]) for axis in range(len(extent))]
    values = values.at[tuple(spot)].set(low)
    longest = extent.index(max(extent))
    spot[longest] = (spot[longest] + 1) % extent[longest]
    return values.at[tuple(spot)].set(largest)


def steps_of(own_key, extent, shards, low, top_value):
    def one(dim, shards_of):
        heights = jax.random.uniform(jax.random.fold_in(jax.random.fold_in(own_key, 6), dim), (shards_of,), jnp.float32, low / len(shards), top_value / len(shards))
        return jnp.repeat(jnp.exp(heights), extent[dim] // shards_of).reshape((-1,) + (1,) * (len(extent) - dim - 1))

    factor_of = one(*shards[0])
    for cut in shards[1:]:
        factor_of = factor_of * one(*cut)
    return factor_of


def centred(key, shape, width, reach, cuts=(), kind=jnp.bfloat16):
    array = jax.random.normal(key, shape, jnp.float32) * width
    if len(cuts) > 0:
        array = steps_of(key, shape, cuts, -0.22, 0.18) * array
    return jnp.clip(array, min=-reach, max=reach).astype(kind)


def setup_inputs(seed: int = 0) -> dict:
    key_of = jax.random.split(jax.random.key(seed), 9)
    return {
        "rhs": draw_rhs(jax.random.fold_in(key_of[8], 71), 0),
        "item_factors": centred(key_of[1], (ITEM_BLOCKS, K, BLOCK), 2048 ** -0.5, 0.125, ((0, 4),)),
        "slot_users": draw_slot_users(jax.random.fold_in(key_of[8], 71), 0),
        "slot_items": draw_slot_items(jax.random.fold_in(key_of[8], 71), 0),
        "slot_counts": draw_slot_counts(jax.random.fold_in(key_of[8], 71), 0),
        "mask_words": plant(jax.random.randint(key_of[5], (GRID_ROWS, GRID_COLS, S_CAP, BLOCK // 8, BLOCK), 0, 256), jax.random.fold_in(key_of[5], 1), 0, 255).astype(jnp.int32),
        "self_tiles": draw_self_tiles(jax.random.fold_in(key_of[8], 71), 0),
        "next_tiles": draw_next_tiles(jax.random.fold_in(key_of[8], 71), 0),
    }


graph_weight = 0.01
ridge_weight = 0.5


def unpack_masks(words):
    shifts = jnp.arange(8, dtype=jnp.int32)
    bits = jnp.right_shift(words[:, :, None, :], shifts[None, None, :, None]) & 1
    return bits.reshape(words.shape[0], words.shape[1] * 8, words.shape[2]).astype(jnp.float32)


def data_term(shared, item_factors, slot_users, slot_items, slot_counts, mask_words):
    grid_rows, grid_cols, capacity = slot_users.shape
    row_blocks = shared.shape[0] // grid_rows
    item_blocks = item_factors.shape[0] // grid_cols
    group = 16 if capacity % 16 == 0 else capacity

    def device(acc, place):
        row_index = place // grid_cols
        col_index = place % grid_cols
        users = (slot_users[row_index, col_index] + row_index * row_blocks).astype(jnp.int32)
        items = (slot_items[row_index, col_index] + col_index * item_blocks).astype(jnp.int32)
        words = mask_words[row_index, col_index]
        count = slot_counts[row_index, col_index]
        trips = (count + group - 1) // group

        def turn(index, inner):
            start = (index * group).astype(jnp.int32)
            part_users = lax.dynamic_slice_in_dim(users, start, group)
            part_items = lax.dynamic_slice_in_dim(items, start, group)
            part_words = lax.dynamic_slice_in_dim(words, start, group)
            valid = ((start + jnp.arange(group, dtype=jnp.int32)) < count).astype(jnp.float32)
            left = item_factors[part_items].astype(jnp.float32)
            right = shared[part_users].astype(jnp.float32)
            scores = jnp.einsum("sdi,sdu->siu", left, right)
            tiles = (scores * unpack_masks(part_words) * valid[:, None, None]).astype(jnp.bfloat16)
            return inner.at[part_users].add(jnp.einsum("siu,sdi->sdu", tiles.astype(jnp.float32), left))

        return lax.fori_loop(0, trips, turn, acc), None

    start_acc = jnp.zeros(shared.shape, jnp.float32)
    places = jnp.arange(grid_rows * grid_cols, dtype=jnp.int32)
    total, unused = lax.scan(device, start_acc, places)
    return total


def graph_term(shared, self_tiles, next_tiles, row_blocks):
    blocks = shared.shape[0]
    local = jnp.arange(blocks, dtype=jnp.int32) % row_blocks
    keep = (local < row_blocks - 1).astype(jnp.float32)
    own = shared.astype(jnp.float32)
    after = jnp.roll(own, -1, axis=0)
    before = jnp.roll(own, 1, axis=0)
    sym = (self_tiles + jnp.swapaxes(self_tiles, 1, 2)).astype(jnp.float32)
    edges = next_tiles.astype(jnp.float32) * keep[:, None, None]
    back = jnp.roll(edges, 1, axis=0)
    degree = jnp.sum(sym, axis=2) + jnp.sum(edges, axis=2) + jnp.sum(back, axis=1)
    result = degree[:, None, :] * own - jnp.einsum("buv,bdv->bdu", sym, own)
    result = result - jnp.einsum("buv,bdv->bdu", edges, after)
    return result - jnp.einsum("buv,bdu->bdv", back, before)


def reference(rhs, item_factors, slot_users, slot_items, slot_counts, mask_words, self_tiles, next_tiles):
    row_blocks = UB_DEV * GRID_COLS

    def apply(vector):
        shared = vector.astype(jnp.bfloat16)
        data = data_term(shared, item_factors, slot_users, slot_items, slot_counts, mask_words)
        graph = graph_term(shared, self_tiles, next_tiles, row_blocks)
        return data + graph_weight * graph + ridge_weight * vector

    solution = jnp.zeros_like(rhs)
    residual = rhs
    direction = rhs
    norm_now = jnp.sum(residual * residual)
    for iteration in range(ITERS):
        image = apply(direction)
        alpha = norm_now / jnp.sum(direction * image)
        solution = solution + alpha * direction
        residual = residual - alpha * image
        norm_next = jnp.sum(residual * residual)
        direction = residual + (norm_next / norm_now) * direction
        norm_now = norm_next
    return solution, residual
```

```python
import functools

import jax
import jax.numpy as jnp
from jax import lax
from jax.experimental import pallas as pl
from jax.experimental.pallas import tpu as pltpu
from jax.sharding import PartitionSpec as P

graph_weight = 0.01
ridge_weight = 0.5
unroll = 16
f32 = jnp.float32
bf16 = jnp.bfloat16

VMEM = pl.BlockSpec(memory_space=pltpu.VMEM)
SMEM = pl.BlockSpec(memory_space=pltpu.SMEM)


def dot(a, b, dims):
    return lax.dot_general(a, b, ((dims[:1], dims[1:]), ((), ())), preferred_element_type=f32)


def add_data(cell, shared, acc):
    users, items, count_ref, factors, words = cell
    count = count_ref[0, 0]
    group = unroll if users.shape[0] % unroll == 0 else 1
    bit = jnp.left_shift(1, lax.broadcasted_iota(jnp.int32, (8, words.shape[2]), 0))

    def turn(index, carry):
        start = index * group
        for step in range(group):
            slot = start + step
            user, item = users[slot], items[slot]
            left = factors[item]
            scores = dot(left, shared[user], (0, 0))
            used = jnp.where(slot < count, bit, 0)
            mask = (words[slot][:, None, :] & used[None]) != 0
            tile = jnp.where(mask.reshape(scores.shape), scores, 0.0).astype(bf16)
            acc[user] += dot(left, tile, (1, 0))
        return carry

    lax.fori_loop(0, (count + group - 1) // group, turn, 0)


def add_graph(tiles, shared, acc, first):
    self_tiles, next_tiles = tiles
    row_blocks = shared.shape[0]
    for j in range(self_tiles.shape[0]):
        local = first + j
        after = jnp.minimum(local + 1, row_blocks - 1)
        keep = (local < row_blocks - 1).astype(f32)
        own, following = shared[local], shared[after]
        weights = self_tiles[j].astype(f32)
        sym = weights + weights.T
        edges = next_tiles[j].astype(f32) * keep
        sym_b, edges_b = sym.astype(bf16), edges.astype(bf16)
        ones = jnp.ones((8, sym.shape[0]), bf16)
        degree = jnp.sum(sym, axis=0, keepdims=True) + dot(ones, edges_b, (1, 1))[:1]
        column_degree = jnp.sum(edges, axis=0, keepdims=True)
        here = degree * own.astype(f32) - dot(own, sym_b, (1, 0)) - dot(following, edges_b, (1, 1))
        there = column_degree * following.astype(f32) - dot(own, edges_b, (1, 0))
        acc[local] += graph_weight * here
        acc[after] += graph_weight * there


def total(value):
    return jnp.sum(jnp.sum(value, axis=tuple(range(value.ndim - 2))), keepdims=True)


def first_kernel(parts, *refs):
    users, items, count, factors, words, self_tiles, next_tiles = refs[:7]
    pieces = refs[7 : 7 + parts]
    acc, shared = refs[7 + parts :]
    me = lax.axis_index("col")
    share = pieces[0].shape[0]
    for offset in range(parts):
        block = (me ^ offset) * share
        shared[pl.ds(block, share)] = pieces[offset][...].astype(bf16)
    acc[...] = jnp.zeros_like(acc)
    add_graph((self_tiles, next_tiles), shared, acc, me * share)
    add_data((users, items, count, factors, words), shared, acc)


def second_kernel(parts, height, *refs):
    users, items, count, factors, words, self_tiles, next_tiles = refs[:7]
    pieces = refs[7 : 7 + parts]
    left, right = refs[7 + parts : 9 + parts]
    outs = refs[9 + parts : 9 + 2 * parts]
    scalars, own_z, own_w, shared, acc, start, image, move = refs[9 + 2 * parts :]
    me, row = lax.axis_index("col"), lax.axis_index("row")
    share = pieces[0].shape[0]
    for offset in range(parts):
        block = (me ^ offset) * share
        start[pl.ds(block, share)] = pieces[offset][...]
    rhs = start[...]
    w = left[...] + right[...] + ridge_weight * rhs
    a, b = total(rhs * rhs), total(rhs * w)
    step = jnp.where(b > 0.0, a / jnp.where(b > 0.0, b, 1.0), 1.0)
    step = jnp.where(step > 0.0, step, 1.0)
    z = rhs - step * w
    image[...] = w
    move[...] = z
    shared[...] = z.astype(bf16)
    rz, zz, zw = total(rhs * z), total(z * z), total(z * w)
    acc[...] = jnp.zeros_like(acc)
    add_graph((self_tiles, next_tiles), shared, acc, me * share)
    add_data((users, items, count, factors, words), shared, acc)
    partial_value = acc[...]
    zh, rh = total(partial_value * move[...]), total(partial_value * start[...])
    part = 1.0 / parts
    values = (
        a * part,
        b * part,
        step * part,
        rz * part,
        zz * part,
        zw * part,
        zh + ridge_weight * part * zz,
        rh + ridge_weight * part * rz,
    )
    lane = lax.broadcasted_iota(jnp.int32, (height, 128), 1)
    sublane = lax.broadcasted_iota(jnp.int32, (height, 128), 0)
    packed = jnp.zeros((height, 128), f32)
    for index, value in enumerate(values):
        packed = jnp.where(lane == index, value, packed)
    scalars[...] = jnp.where(sublane == row, packed, 0.0)
    for offset in range(parts):
        outs[offset][...] = acc[pl.ds((me ^ offset) * share, share)]
    own_z[...] = move[pl.ds(me * share, share)]
    own_w[...] = image[pl.ds(me * share, share)]


def last_kernel(parts, scalar_parts, *refs):
    own_r, own_z, own_w = refs[:3]
    images = refs[3 : 3 + parts]
    scalars = refs[3 + parts : 3 + parts + scalar_parts]
    solution_ref, residual_ref = refs[3 + parts + scalar_parts :]
    table = scalars[0][...]
    for ref in scalars[1:]:
        table = table + ref[...]
    row = lax.axis_index("row")
    height = table.shape[0]
    a, b, step, rz, zz, zw, zh, rh = (table[:, k : k + 1] for k in range(8))

    def whole(value):
        return jnp.sum(value, axis=0, keepdims=True)

    norm = whole(a)
    alpha = norm / whole(b)
    rho = alpha / jnp.where(step > 0.0, step, 1.0)
    rest = 1.0 - rho
    norm_next = whole(rest * rest * a + 2.0 * rest * rho * rz + rho * rho * zz)
    beta = norm_next / norm
    p = rest + beta
    curve = whole(p * p * b + p * rho * (zw + rh) + rho * rho * zh)
    alpha_next = norm_next / curve
    sublane = lax.broadcasted_iota(jnp.int32, (height, 1), 0)
    mine = jnp.where(sublane == row, rho, 0.0)
    rho = whole(mine)
    rest = 1.0 - rho
    p = rest + beta
    r, z, w = own_r[...], own_z[...], own_w[...]
    hz = ridge_weight * z
    for ref in images:
        hz = hz + ref[...]
    solution_ref[...] = (alpha + alpha_next * p) * r + (alpha_next * rho) * z
    residual_ref[...] = rest * r + rho * z - alpha_next * (p * w + rho * hz)


def exchange(value, axes, size, offset):
    return lax.ppermute(value, axes, [(i, i ^ offset) for i in range(size)])


def bit_groups(size):
    bits = [1 << k for k in range(size.bit_length() - 1)]
    groups = [bits[:1]] + [bits[k : k + 2] for k in range(1, len(bits), 2)]
    return [group for group in groups if group]


def spans(group):
    offsets = [0]
    for bit in group:
        offsets = offsets + [offset ^ bit for offset in offsets]
    return offsets[1:]


def per_device(
    rows, cols, rhs, item_factors, slot_users, slot_items, slot_counts, mask_words, self_tiles, next_tiles
):
    share, rank, width = rhs.shape
    row_shape = (cols * share, rank, width)
    cell = (
        slot_users[0, 0],
        slot_items[0, 0],
        slot_counts,
        item_factors,
        mask_words[0, 0],
        self_tiles,
        next_tiles,
    )
    cell_specs = [SMEM] * 3 + [VMEM] * 4
    params = pltpu.CompilerParams(vmem_limit_bytes=40 * 1024 * 1024)
    pieces = [rhs] + [exchange(rhs, "col", cols, offset) for offset in range(1, cols)]

    value = pl.pallas_call(
        functools.partial(first_kernel, cols),
        out_shape=jax.ShapeDtypeStruct(row_shape, f32),
        in_specs=cell_specs + [VMEM] * cols,
        out_specs=VMEM,
        scratch_shapes=[pltpu.VMEM(row_shape, bf16)],
        compiler_params=params,
        name="first_apply",
    )(*cell, *pieces)
    bits = [1 << k for k in range(cols.bit_length() - 1)]
    other = jnp.zeros_like(value) if not bits else None
    for index, bit in enumerate(bits):
        other = exchange(value, "col", cols, bit)
        if index + 1 < len(bits):
            value = value + other

    height = -(-rows // 8) * 8
    piece = jax.ShapeDtypeStruct(rhs.shape, f32)
    outs = pl.pallas_call(
        functools.partial(second_kernel, cols, height),
        out_shape=[piece] * cols + [jax.ShapeDtypeStruct((height, 128), f32), piece, piece],
        in_specs=cell_specs + [VMEM] * (cols + 2),
        out_specs=[VMEM] * (cols + 3),
        scratch_shapes=[pltpu.VMEM(row_shape, bf16)] + [pltpu.VMEM(row_shape, f32)] * 4,
        compiler_params=params,
        name="second_apply",
    )(*cell, *pieces, value, other)
    table, own_z, own_w = outs[cols:]
    images = [outs[0]] + [exchange(outs[offset], "col", cols, offset) for offset in range(1, cols)]
    groups = bit_groups(rows * cols)
    tables = [table]
    for group in groups:
        table = functools.reduce(jnp.add, tables)
        tables = [table] + [exchange(table, ("row", "col"), rows * cols, o) for o in spans(group)]

    return pl.pallas_call(
        functools.partial(last_kernel, cols, len(tables)),
        out_shape=[piece, piece],
        in_specs=[VMEM] * (3 + cols + len(tables)),
        out_specs=[VMEM] * 2,
        compiler_params=params,
        name="last_update",
    )(rhs, own_z, own_w, *images, *tables)


def solution(mesh):
    rows, cols = mesh.shape["row"], mesh.shape["col"]
    return jax.shard_map(
        functools.partial(per_device, rows, cols),
        mesh=mesh,
        in_specs=(
            P(("row", "col"), None, None),
            P("col", None, None),
            P("row", "col", None),
            P("row", "col", None),
            P("row", "col"),
            P("row", "col", None, None, None),
            P(("row", "col"), None, None),
            P(("row", "col"), None, None),
        ),
        out_specs=(P(("row", "col"), None, None), P(("row", "col"), None, None)),
        check_vma=False,
    )
```

```python
import functools

import jax
import jax.numpy as jnp
from jax import lax
from jax.experimental import pallas as pl
from jax.experimental.pallas import tpu as pltpu
from jax.sharding import PartitionSpec as P

graph_weight = 0.01
ridge_weight = 0.5
unroll = 16
f32 = jnp.float32
bf16 = jnp.bfloat16

VMEM = pl.BlockSpec(memory_space=pltpu.VMEM)
HBM = pl.BlockSpec(memory_space=pltpu.HBM)
SMEM = pl.BlockSpec(memory_space=pltpu.SMEM)


def dot(a, b, dims):
    return lax.dot_general(a, b, ((dims[:1], dims[1:]), ((), ())), preferred_element_type=f32)


def add_data(cell, shared, acc):
    users, items, count_ref, factors, words = cell
    count = count_ref[0, 0]
    group = unroll if users.shape[0] % unroll == 0 else 1
    bit = jnp.left_shift(1, lax.broadcasted_iota(jnp.int32, (8, words.shape[2]), 0))

    def turn(index, carry):
        start = index * group
        for step in range(group):
            slot = start + step
            user, item = users[slot], items[slot]
            left = factors[item]
            scores = dot(left, shared[user], (0, 0))
            used = jnp.where(slot < count, bit, 0)
            mask = (words[slot][:, None, :] & used[None]) != 0
            tile = jnp.where(mask.reshape(scores.shape), scores, 0.0).astype(bf16)
            acc[user] += dot(left, tile, (1, 0))
        return carry

    lax.fori_loop(0, (count + group - 1) // group, turn, 0)


def add_graph(graph, shared, acc, first):
    sym, edges, degrees = graph
    row_blocks = shared.shape[0]
    for j in range(sym.shape[0]):
        local = first + j
        after = jnp.minimum(local + 1, row_blocks - 1)
        own, following = shared[local], shared[after]
        degree, column_degree = degrees[j, 0:1], degrees[j, 8:9]
        here = degree * own.astype(f32) - dot(own, sym[j], (1, 0)) - dot(following, edges[j], (1, 1))
        there = column_degree * following.astype(f32) - dot(own, edges[j], (1, 0))
        acc[local] += graph_weight * here
        acc[after] += graph_weight * there


def prepare_kernel(cols, factors_in, words_in, self_in, next_in, factors, words, sym, edges, degrees, tiles, sems):
    first = lax.axis_index("col") * self_in.shape[0]
    copies = [
        pltpu.make_async_copy(source, target, sems.at[k])
        for k, (source, target) in enumerate(
            ((self_in, tiles.at[0]), (next_in, tiles.at[1]), (factors_in, factors), (words_in, words))
        )
    ]
    for copy in copies:
        copy.start()
    copies[0].wait()
    copies[1].wait()
    count = self_in.shape[0]
    for j in range(count):
        keep = (first + j < cols * count - 1).astype(f32)
        weights = tiles[0, j].astype(f32)
        both = weights + weights.T
        edge = tiles[1, j].astype(f32) * keep
        edges_b = edge.astype(bf16)
        sym[j] = both.astype(bf16)
        edges[j] = edges_b
        ones = jnp.ones((8, both.shape[0]), bf16)
        degrees[j, 0:8] = jnp.sum(both, axis=0, keepdims=True) + dot(ones, edges_b, (1, 1))
        degrees[j, 8:16] = jnp.broadcast_to(jnp.sum(edge, axis=0, keepdims=True), (8, both.shape[1]))
    copies[2].wait()
    copies[3].wait()


def total(value):
    return jnp.sum(jnp.sum(value, axis=tuple(range(value.ndim - 2))), keepdims=True)


def first_kernel(parts, *refs):
    users, items, count, factors, words, sym, edges, degrees = refs[:8]
    pieces = refs[8 : 8 + parts]
    keep, send, shared, acc = refs[8 + parts :]
    me = lax.axis_index("col")
    share = pieces[0].shape[0]
    for offset in range(parts):
        block = (me ^ offset) * share
        shared[pl.ds(block, share)] = pieces[offset][...].astype(bf16)
    acc[...] = jnp.zeros_like(acc)
    add_graph((sym, edges, degrees), shared, acc, me * share)
    add_data((users, items, count, factors, words), shared, acc)
    split(acc, keep, send, me, share)


def split(acc, keep, send, me, share):
    odd = me & 1
    for j in range(keep.shape[0] // share):
        keep[pl.ds(j * share, share)] = acc[pl.ds((2 * j + odd) * share, share)]
        send[pl.ds(j * share, share)] = acc[pl.ds((2 * j + (odd ^ 1)) * share, share)]


def second_kernel(parts, height, *refs):
    users, items, count, factors, words, sym, edges, degrees = refs[:8]
    pieces = refs[8 : 8 + parts]
    mine, theirs = refs[8 + parts : 10 + parts]
    keep, send, scalars, own_z, own_w, shared, acc, start, image, move = refs[10 + parts :]
    me, row = lax.axis_index("col"), lax.axis_index("row")
    share = pieces[0].shape[0]
    for offset in range(parts):
        block = (me ^ offset) * share
        start[pl.ds(block, share)] = pieces[offset][...]
    odd = me & 1
    for j in range(parts // 2):
        image[pl.ds((2 * j + odd) * share, share)] = mine[pl.ds(j * share, share)]
        image[pl.ds((2 * j + (odd ^ 1)) * share, share)] = theirs[pl.ds(j * share, share)]
    rhs = start[...]
    w = image[...] + ridge_weight * rhs
    a, b = total(rhs * rhs), total(rhs * w)
    step = jnp.where(b > 0.0, a / jnp.where(b > 0.0, b, 1.0), 1.0)
    step = jnp.where(step > 0.0, step, 1.0)
    z = rhs - step * w
    image[...] = w
    move[...] = z
    shared[...] = z.astype(bf16)
    rz, zz, zw = total(rhs * z), total(z * z), total(z * w)
    acc[...] = jnp.zeros_like(acc)
    add_graph((sym, edges, degrees), shared, acc, me * share)
    add_data((users, items, count, factors, words), shared, acc)
    partial_value = acc[...]
    zh, rh = total(partial_value * move[...]), total(partial_value * start[...])
    part = 1.0 / parts
    values = (
        a * part,
        b * part,
        step * part,
        rz * part,
        zz * part,
        zw * part,
        zh + ridge_weight * part * zz,
        rh + ridge_weight * part * rz,
    )
    lane = lax.broadcasted_iota(jnp.int32, (height, 128), 1)
    sublane = lax.broadcasted_iota(jnp.int32, (height, 128), 0)
    packed = jnp.zeros((height, 128), f32)
    for index, value in enumerate(values):
        packed = jnp.where(lane == index, value, packed)
    scalars[...] = jnp.where(sublane == row, packed, 0.0)
    for j in range(parts // 2):
        keep[pl.ds(j * share, share)] = acc[pl.ds((me ^ (2 * j)) * share, share)]
        send[pl.ds(j * share, share)] = acc[pl.ds((me ^ (2 * j + 1)) * share, share)]
    own_z[...] = move[pl.ds(me * share, share)]
    own_w[...] = image[pl.ds(me * share, share)]


def last_kernel(parts, scalar_parts, *refs):
    own_r, own_z, own_w = refs[:3]
    images = refs[3 : 3 + parts]
    scalars = refs[3 + parts : 3 + parts + scalar_parts]
    solution_ref, residual_ref = refs[3 + parts + scalar_parts :]
    table = scalars[0][...]
    for ref in scalars[1:]:
        table = table + ref[...]
    row = lax.axis_index("row")
    height = table.shape[0]
    a, b, step, rz, zz, zw, zh, rh = (table[:, k : k + 1] for k in range(8))

    def whole(value):
        return jnp.sum(value, axis=0, keepdims=True)

    norm = whole(a)
    alpha = norm / whole(b)
    rho = alpha / jnp.where(step > 0.0, step, 1.0)
    rest = 1.0 - rho
    norm_next = whole(rest * rest * a + 2.0 * rest * rho * rz + rho * rho * zz)
    beta = norm_next / norm
    p = rest + beta
    curve = whole(p * p * b + p * rho * (zw + rh) + rho * rho * zh)
    alpha_next = norm_next / curve
    sublane = lax.broadcasted_iota(jnp.int32, (height, 1), 0)
    mine = jnp.where(sublane == row, rho, 0.0)
    rho = whole(mine)
    rest = 1.0 - rho
    p = rest + beta
    r, z, w = own_r[...], own_z[...], own_w[...]
    hz = ridge_weight * z
    for ref in images:
        hz = hz + ref[: z.shape[0]]
    solution_ref[...] = (alpha + alpha_next * p) * r + (alpha_next * rho) * z
    residual_ref[...] = rest * r + rho * z - alpha_next * (p * w + rho * hz)


def exchange(value, axes, size, offset):
    return lax.ppermute(value, axes, [(i, i ^ offset) for i in range(size)])


def bit_groups(size):
    bits = [1 << k for k in range(size.bit_length() - 1)]
    groups = [bits[:1]] + [bits[k : k + 2] for k in range(1, len(bits), 2)]
    return [group for group in groups if group]


def spans(group):
    offsets = [0]
    for bit in group:
        offsets = offsets + [offset ^ bit for offset in offsets]
    return offsets[1:]


def per_device(
    rows, cols, rhs, item_factors, slot_users, slot_items, slot_counts, mask_words, self_tiles, next_tiles
):
    share, rank, width = rhs.shape
    row_shape = (cols * share, rank, width)
    half = jax.ShapeDtypeStruct((cols * share // 2, rank, width), f32)
    piece = jax.ShapeDtypeStruct(rhs.shape, f32)
    params = pltpu.CompilerParams(vmem_limit_bytes=40 * 1024 * 1024)
    pieces = [rhs] + [exchange(rhs, "col", cols, offset) for offset in range(1, cols)]
    words = mask_words[0, 0]
    tile_shape = self_tiles.shape

    factors, words, sym, edges, degrees = pl.pallas_call(
        functools.partial(prepare_kernel, cols),
        out_shape=[
            jax.ShapeDtypeStruct(item_factors.shape, bf16),
            jax.ShapeDtypeStruct(words.shape, words.dtype),
            jax.ShapeDtypeStruct(tile_shape, bf16),
            jax.ShapeDtypeStruct(tile_shape, bf16),
            jax.ShapeDtypeStruct((tile_shape[0], 16, tile_shape[2]), f32),
        ],
        in_specs=[HBM] * 4,
        out_specs=[VMEM] * 5,
        scratch_shapes=[pltpu.VMEM((2,) + tile_shape, jnp.int32), pltpu.SemaphoreType.DMA((4,))],
        compiler_params=params,
        cost_estimate=pl.CostEstimate(flops=10**6, bytes_accessed=4 * 10**6, transcendentals=0),
        name="prepare",
    )(*(pltpu.with_memory_space_constraint(x, pltpu.HBM) for x in (item_factors, words, self_tiles, next_tiles)))
    cell = (slot_users[0, 0], slot_items[0, 0], slot_counts, factors, words, sym, edges, degrees)
    cell_specs = [SMEM] * 3 + [VMEM] * 5

    keep, send = pl.pallas_call(
        functools.partial(first_kernel, cols),
        out_shape=[half, half],
        in_specs=cell_specs + [VMEM] * cols,
        out_specs=[VMEM] * 2,
        scratch_shapes=[pltpu.VMEM(row_shape, bf16), pltpu.VMEM(row_shape, f32)],
        compiler_params=params,
        name="first_apply",
    )(*cell, *pieces)
    keep = keep + exchange(send, "col", cols, 1)
    bits = [1 << k for k in range(1, cols.bit_length() - 1)]
    for bit in bits:
        keep = keep + exchange(keep, "col", cols, bit)
    theirs = exchange(keep, "col", cols, 1)

    height = -(-rows // 8) * 8
    keep, send, table, own_z, own_w = pl.pallas_call(
        functools.partial(second_kernel, cols, height),
        out_shape=[half, half, jax.ShapeDtypeStruct((height, 128), f32), piece, piece],
        in_specs=cell_specs + [VMEM] * (cols + 2),
        out_specs=[VMEM] * 5,
        scratch_shapes=[pltpu.VMEM(row_shape, bf16)] + [pltpu.VMEM(row_shape, f32)] * 4,
        compiler_params=params,
        name="second_apply",
    )(*cell, *pieces, keep, theirs)
    pair = exchange(send, "col", cols, 1)
    images = [keep, pair]
    for j in range(1, cols // 2):
        block = slice(j * share, (j + 1) * share)
        images.append(exchange(keep[block] + pair[block], "col", cols, 2 * j))
    tables = [table]
    for group in bit_groups(rows * cols):
        table = functools.reduce(jnp.add, tables)
        tables = [table] + [exchange(table, ("row", "col"), rows * cols, o) for o in spans(group)]

    return pl.pallas_call(
        functools.partial(last_kernel, len(images), len(tables)),
        out_shape=[piece, piece],
        in_specs=[VMEM] * (3 + len(images) + len(tables)),
        out_specs=[VMEM] * 2,
        compiler_params=params,
        name="last_update",
    )(rhs, own_z, own_w, *images, *tables)


def solution(mesh):
    rows, cols = mesh.shape["row"], mesh.shape["col"]
    return jax.shard_map(
        functools.partial(per_device, rows, cols),
        mesh=mesh,
        in_specs=(
            P(("row", "col"), None, None),
            P("col", None, None),
            P("row", "col", None),
            P("row", "col", None),
            P("row", "col"),
            P("row", "col", None, None, None),
            P(("row", "col"), None, None),
            P(("row", "col"), None, None),
        ),
        out_specs=(P(("row", "col"), None, None), P(("row", "col"), None, None)),
        check_vma=False,
    )
```

```python
import functools

import jax
import jax.numpy as jnp
from jax import lax
from jax.experimental import pallas as pl
from jax.experimental.pallas import tpu as pltpu
from jax.sharding import PartitionSpec as P

graph_weight = 0.01
ridge_weight = 0.5
unroll = 96
f32 = jnp.float32
bf16 = jnp.bfloat16

VMEM = pl.BlockSpec(memory_space=pltpu.VMEM)
HBM = pl.BlockSpec(memory_space=pltpu.HBM)
SMEM = pl.BlockSpec(memory_space=pltpu.SMEM)


def dot(a, b, dims):
    return lax.dot_general(a, b, ((dims[:1], dims[1:]), ((), ())), preferred_element_type=f32)


def add_data(cell, shared, acc):
    users, items, count_ref, factors, words = cell
    count = count_ref[0, 0]
    slots = users.shape[0]
    group = max(k for k in range(1, unroll + 1) if slots % k == 0)
    bit = jnp.left_shift(1, lax.broadcasted_iota(jnp.int32, (8, words.shape[2]), 0))

    def turn(index, carry):
        start = index * group
        for step in range(group):
            slot = start + step
            user, item = users[slot], items[slot]
            left = factors[item]
            scores = dot(left, shared[user], (0, 0))
            used = jnp.where(slot < count, bit, 0)
            mask = (words[slot][:, None, :] & used[None]) != 0
            tile = jnp.where(mask.reshape(scores.shape), scores, 0.0).astype(bf16)
            acc[user] += dot(left, tile, (1, 0))
        return carry

    if group == slots:
        turn(0, 0)
    else:
        lax.fori_loop(0, (count + group - 1) // group, turn, 0)


def add_graph(graph, shared, acc, first):
    sym, edges, degrees = graph
    row_blocks = shared.shape[0]
    for j in range(sym.shape[0]):
        local = first + j
        after = jnp.minimum(local + 1, row_blocks - 1)
        own, following = shared[local], shared[after]
        degree, column_degree = degrees[j, 0:1], degrees[j, 8:9]
        here = degree * own.astype(f32) - dot(own, sym[j], (1, 0)) - dot(following, edges[j], (1, 1))
        there = column_degree * following.astype(f32) - dot(own, edges[j], (1, 0))
        acc[local] += graph_weight * here
        acc[after] += graph_weight * there


def prepare_kernel(cols, *refs):
    factors_in, words_in, users_in, items_in, self_in, next_in = refs[:6]
    factors, words, users, items, sym, edges, degrees, tiles, sems = refs[6:]
    first = lax.axis_index("col") * self_in.shape[0]
    copies = [
        pltpu.make_async_copy(source, target, sems.at[k])
        for k, (source, target) in enumerate(
            (
                (self_in, tiles.at[0]),
                (next_in, tiles.at[1]),
                (factors_in, factors),
                (words_in, words),
                (users_in, users),
                (items_in, items),
            )
        )
    ]
    for copy in copies:
        copy.start()
    copies[0].wait()
    copies[1].wait()
    count = self_in.shape[0]
    for j in range(count):
        keep = (first + j < cols * count - 1).astype(f32)
        weights = tiles[0, j].astype(f32)
        both = weights + weights.T
        edge = tiles[1, j].astype(f32) * keep
        edges_b = edge.astype(bf16)
        sym[j] = both.astype(bf16)
        edges[j] = edges_b
        ones = jnp.ones((8, both.shape[0]), bf16)
        degrees[j, 0:8] = jnp.sum(both, axis=0, keepdims=True) + dot(ones, edges_b, (1, 1))
        degrees[j, 8:16] = jnp.broadcast_to(jnp.sum(edge, axis=0, keepdims=True), (8, both.shape[1]))
    for copy in copies[2:]:
        copy.wait()


def total(value):
    return jnp.sum(jnp.sum(value, axis=tuple(range(value.ndim - 2))), keepdims=True)


def first_kernel(parts, *refs):
    users, items, count, factors, words, sym, edges, degrees = refs[:8]
    pieces = refs[8 : 8 + parts]
    keep, send, shared, acc = refs[8 + parts :]
    me = lax.axis_index("col")
    share = pieces[0].shape[0]
    for offset in range(parts):
        block = (me ^ offset) * share
        shared[pl.ds(block, share)] = pieces[offset][...].astype(bf16)
    acc[...] = jnp.zeros_like(acc)
    add_graph((sym, edges, degrees), shared, acc, me * share)
    add_data((users, items, count, factors, words), shared, acc)
    split(acc, keep, send, me, share)


def split(acc, keep, send, me, share):
    odd = me & 1
    for j in range(keep.shape[0] // share):
        keep[pl.ds(j * share, share)] = acc[pl.ds((2 * j + odd) * share, share)]
        send[pl.ds(j * share, share)] = acc[pl.ds((2 * j + (odd ^ 1)) * share, share)]


def second_kernel(parts, height, *refs):
    users, items, count, factors, words, sym, edges, degrees = refs[:8]
    pieces = refs[8 : 8 + parts]
    mine, theirs = refs[8 + parts : 10 + parts]
    keep, send, scalars, own_z, own_w, shared, acc, start, image, move = refs[10 + parts :]
    me, row = lax.axis_index("col"), lax.axis_index("row")
    share = pieces[0].shape[0]
    for offset in range(parts):
        block = (me ^ offset) * share
        start[pl.ds(block, share)] = pieces[offset][...]
    odd = me & 1
    for j in range(parts // 2):
        image[pl.ds((2 * j + odd) * share, share)] = mine[pl.ds(j * share, share)]
        image[pl.ds((2 * j + (odd ^ 1)) * share, share)] = theirs[pl.ds(j * share, share)]
    rhs = start[...]
    w = image[...] + ridge_weight * rhs
    a, b = total(rhs * rhs), total(rhs * w)
    step = jnp.where(b > 0.0, a / jnp.where(b > 0.0, b, 1.0), 1.0)
    step = jnp.where(step > 0.0, step, 1.0)
    z = rhs - step * w
    image[...] = w
    move[...] = z
    shared[...] = z.astype(bf16)
    rz, zz, zw = total(rhs * z), total(z * z), total(z * w)
    acc[...] = jnp.zeros_like(acc)
    add_graph((sym, edges, degrees), shared, acc, me * share)
    add_data((users, items, count, factors, words), shared, acc)
    partial_value = acc[...]
    zh, rh = total(partial_value * move[...]), total(partial_value * start[...])
    part = 1.0 / parts
    values = (
        a * part,
        b * part,
        step * part,
        rz * part,
        zz * part,
        zw * part,
        zh + ridge_weight * part * zz,
        rh + ridge_weight * part * rz,
    )
    lane = lax.broadcasted_iota(jnp.int32, (height, 128), 1)
    sublane = lax.broadcasted_iota(jnp.int32, (height, 128), 0)
    packed = jnp.zeros((height, 128), f32)
    for index, value in enumerate(values):
        packed = jnp.where(lane == index, value, packed)
    scalars[...] = jnp.where(sublane == row, packed, 0.0)
    for j in range(parts // 2):
        keep[pl.ds(j * share, share)] = acc[pl.ds((me ^ (2 * j)) * share, share)]
        send[pl.ds(j * share, share)] = acc[pl.ds((me ^ (2 * j + 1)) * share, share)]
    own_z[...] = move[pl.ds(me * share, share)]
    own_w[...] = image[pl.ds(me * share, share)]


def last_kernel(parts, scalar_parts, *refs):
    own_r, own_z, own_w = refs[:3]
    images = refs[3 : 3 + parts]
    scalars = refs[3 + parts : 3 + parts + scalar_parts]
    solution_ref, residual_ref = refs[3 + parts + scalar_parts :]
    table = scalars[0][...]
    for ref in scalars[1:]:
        table = table + ref[...]
    row = lax.axis_index("row")
    height = table.shape[0]
    a, b, step, rz, zz, zw, zh, rh = (table[:, k : k + 1] for k in range(8))

    def whole(value):
        return jnp.sum(value, axis=0, keepdims=True)

    norm = whole(a)
    alpha = norm / whole(b)
    rho = alpha / jnp.where(step > 0.0, step, 1.0)
    rest = 1.0 - rho
    norm_next = whole(rest * rest * a + 2.0 * rest * rho * rz + rho * rho * zz)
    beta = norm_next / norm
    p = rest + beta
    curve = whole(p * p * b + p * rho * (zw + rh) + rho * rho * zh)
    alpha_next = norm_next / curve
    sublane = lax.broadcasted_iota(jnp.int32, (height, 1), 0)
    mine = jnp.where(sublane == row, rho, 0.0)
    rho = whole(mine)
    rest = 1.0 - rho
    p = rest + beta
    r, z, w = own_r[...], own_z[...], own_w[...]
    hz = ridge_weight * z
    for ref in images:
        hz = hz + ref[: z.shape[0]]
    solution_ref[...] = (alpha + alpha_next * p) * r + (alpha_next * rho) * z
    residual_ref[...] = rest * r + rho * z - alpha_next * (p * w + rho * hz)


def exchange(value, axes, size, offset):
    return lax.ppermute(value, axes, [(i, i ^ offset) for i in range(size)])


def bit_groups(size):
    bits = [1 << k for k in range(size.bit_length() - 1)]
    groups = [bits[:1]] + [bits[k : k + 2] for k in range(1, len(bits), 2)]
    return [group for group in groups if group]


def spans(group):
    offsets = [0]
    for bit in group:
        offsets = offsets + [offset ^ bit for offset in offsets]
    return offsets[1:]


def per_device(
    rows, cols, rhs, item_factors, slot_users, slot_items, slot_counts, mask_words, self_tiles, next_tiles
):
    share, rank, width = rhs.shape
    row_shape = (cols * share, rank, width)
    half = jax.ShapeDtypeStruct((cols * share // 2, rank, width), f32)
    piece = jax.ShapeDtypeStruct(rhs.shape, f32)
    params = pltpu.CompilerParams(vmem_limit_bytes=40 * 1024 * 1024)
    pieces = [rhs] + [exchange(rhs, "col", cols, offset) for offset in range(1, cols)]
    words = mask_words[0, 0]
    tile_shape = self_tiles.shape

    users, items = slot_users[0, 0], slot_items[0, 0]
    factors, words, users, items, sym, edges, degrees = pl.pallas_call(
        functools.partial(prepare_kernel, cols),
        out_shape=[
            jax.ShapeDtypeStruct(item_factors.shape, bf16),
            jax.ShapeDtypeStruct(words.shape, words.dtype),
            jax.ShapeDtypeStruct(users.shape, users.dtype),
            jax.ShapeDtypeStruct(items.shape, items.dtype),
            jax.ShapeDtypeStruct(tile_shape, bf16),
            jax.ShapeDtypeStruct(tile_shape, bf16),
            jax.ShapeDtypeStruct((tile_shape[0], 16, tile_shape[2]), f32),
        ],
        in_specs=[HBM] * 6,
        out_specs=[VMEM] * 2 + [SMEM] * 2 + [VMEM] * 3,
        scratch_shapes=[pltpu.VMEM((2,) + tile_shape, jnp.int32), pltpu.SemaphoreType.DMA((6,))],
        compiler_params=params,
        cost_estimate=pl.CostEstimate(flops=10**6, bytes_accessed=4 * 10**6, transcendentals=0),
        name="prepare",
    )(*(pltpu.with_memory_space_constraint(x, pltpu.HBM) for x in (item_factors, words, users, items, self_tiles, next_tiles)))
    cell = (users, items, slot_counts, factors, words, sym, edges, degrees)
    cell_specs = [SMEM] * 3 + [VMEM] * 5

    keep, send = pl.pallas_call(
        functools.partial(first_kernel, cols),
        out_shape=[half, half],
        in_specs=cell_specs + [VMEM] * cols,
        out_specs=[VMEM] * 2,
        scratch_shapes=[pltpu.VMEM(row_shape, bf16), pltpu.VMEM(row_shape, f32)],
        compiler_params=params,
        name="first_apply",
    )(*cell, *pieces)
    keep = keep + exchange(send, "col", cols, 1)
    bits = [1 << k for k in range(1, cols.bit_length() - 1)]
    for bit in bits:
        keep = keep + exchange(keep, "col", cols, bit)
    theirs = exchange(keep, "col", cols, 1)

    height = -(-rows // 8) * 8
    keep, send, table, own_z, own_w = pl.pallas_call(
        functools.partial(second_kernel, cols, height),
        out_shape=[half, half, jax.ShapeDtypeStruct((height, 128), f32), piece, piece],
        in_specs=cell_specs + [VMEM] * (cols + 2),
        out_specs=[VMEM] * 5,
        scratch_shapes=[pltpu.VMEM(row_shape, bf16)] + [pltpu.VMEM(row_shape, f32)] * 4,
        compiler_params=params,
        name="second_apply",
    )(*cell, *pieces, keep, theirs)
    pair = exchange(send, "col", cols, 1)
    images = [keep, pair]
    for j in range(1, cols // 2):
        block = slice(j * share, (j + 1) * share)
        images.append(exchange(keep[block] + pair[block], "col", cols, 2 * j))
    tables = [table]
    for group in bit_groups(rows * cols):
        table = functools.reduce(jnp.add, tables)
        tables = [table] + [exchange(table, ("row", "col"), rows * cols, o) for o in spans(group)]

    return pl.pallas_call(
        functools.partial(last_kernel, len(images), len(tables)),
        out_shape=[piece, piece],
        in_specs=[VMEM] * (3 + len(images) + len(tables)),
        out_specs=[VMEM] * 2,
        compiler_params=params,
        name="last_update",
    )(rhs, own_z, own_w, *images, *tables)


def solution(mesh):
    rows, cols = mesh.shape["row"], mesh.shape["col"]
    return jax.shard_map(
        functools.partial(per_device, rows, cols),
        mesh=mesh,
        in_specs=(
            P(("row", "col"), None, None),
            P("col", None, None),
            P("row", "col", None),
            P("row", "col", None),
            P("row", "col"),
            P("row", "col", None, None, None),
            P(("row", "col"), None, None),
            P(("row", "col"), None, None),
        ),
        out_specs=(P(("row", "col"), None, None), P(("row", "col"), None, None)),
        check_vma=False,
    )
```

```python
import functools

import jax
import jax.numpy as jnp
from jax import lax
from jax.experimental import pallas as pl
from jax.experimental.pallas import tpu as pltpu
from jax.sharding import PartitionSpec as P

graph_weight = 0.01
ridge_weight = 0.5
unroll = 96
f32 = jnp.float32
bf16 = jnp.bfloat16

VMEM = pl.BlockSpec(memory_space=pltpu.VMEM)
HBM = pl.BlockSpec(memory_space=pltpu.HBM)
SMEM = pl.BlockSpec(memory_space=pltpu.SMEM)


def dot(a, b, dims):
    return lax.dot_general(a, b, ((dims[:1], dims[1:]), ((), ())), preferred_element_type=f32)


def add_data(cell, shared, acc):
    users, items, count_ref, factors, words = cell
    count = count_ref[0, 0]
    slots = users.shape[1]
    group = max(k for k in range(1, unroll + 1) if slots % k == 0)
    bit = jnp.left_shift(1, lax.broadcasted_iota(jnp.int32, (8, words.shape[2]), 0))

    def turn(index, carry):
        start = index * group
        for step in range(group):
            slot = start + step
            user, item = users[0, slot], items[0, slot]
            left = factors[item]
            pieces = shared.shape[1] // left.shape[0]
            scores = dot(jnp.concatenate([left] * pieces), shared[user], (0, 0))
            used = jnp.where(slot < count, bit, 0)
            mask = (words[slot][:, None, :] & used[None]) != 0
            tile = jnp.where(mask.reshape(scores.shape), scores, 0.0).astype(bf16)
            acc[user] += dot(left, tile, (1, 0))
        return carry

    if group == slots:
        turn(0, 0)
    else:
        lax.fori_loop(0, (count + group - 1) // group, turn, 0)


def add_graph(graph, shared, acc, first):
    sym, edges, degrees = graph
    row_blocks = shared.shape[0]
    for j in range(sym.shape[0]):
        local = first + j
        after = jnp.minimum(local + 1, row_blocks - 1)
        own, following = shared[local], shared[after]
        degree, column_degree = degrees[j, 0:1], degrees[j, 8:9]
        here = degree * own.astype(f32) - dot(own, sym[j], (1, 0)) - dot(following, edges[j], (1, 1))
        there = column_degree * following.astype(f32) - dot(own, edges[j], (1, 0))
        rank = acc.shape[1]
        here = sum(here[k : k + rank] for k in range(0, here.shape[0], rank))
        there = sum(there[k : k + rank] for k in range(0, there.shape[0], rank))
        acc[local] += graph_weight * here
        acc[after] += graph_weight * there


def prepare_kernel(cols, *refs):
    factors_in, words_in, users_in, items_in, self_in, next_in = refs[:6]
    factors, words, users, items, sym, edges, degrees, tiles, sems = refs[6:]
    first = lax.axis_index("col") * self_in.shape[0]
    copies = [
        pltpu.make_async_copy(source, target, sems.at[k])
        for k, (source, target) in enumerate(
            (
                (self_in, tiles.at[0]),
                (next_in, tiles.at[1]),
                (factors_in, factors),
                (words_in, words),
                (users_in, users),
                (items_in, items),
            )
        )
    ]
    for copy in copies:
        copy.start()
    copies[0].wait()
    copies[1].wait()
    count = self_in.shape[0]
    for j in range(count):
        keep = (first + j < cols * count - 1).astype(f32)
        weights = tiles[0, j].astype(f32)
        both = weights + weights.T
        edge = tiles[1, j].astype(f32) * keep
        edges_b = edge.astype(bf16)
        sym[j] = both.astype(bf16)
        edges[j] = edges_b
        ones = jnp.ones((8, both.shape[0]), bf16)
        degrees[j, 0:8] = jnp.sum(both, axis=0, keepdims=True) + dot(ones, edges_b, (1, 1))
        degrees[j, 8:16] = jnp.broadcast_to(jnp.sum(edge, axis=0, keepdims=True), (8, both.shape[1]))
    for copy in copies[2:]:
        copy.wait()


def even_masks(cols):
    return [mask for mask in range(cols) if bin(mask).count("1") % 2 == 0]


def total(value):
    return jnp.sum(jnp.sum(value, axis=tuple(range(value.ndim - 2))), keepdims=True)


def first_kernel(parts, *refs):
    users, items, count, factors, words, sym, edges, degrees = refs[:8]
    pieces = refs[8 : 8 + parts]
    acc, shared = refs[8 + parts :]
    me = lax.axis_index("col")
    share = pieces[0].shape[0]
    for offset in range(parts):
        block = (me ^ offset) * share
        shared[pl.ds(block, share)] = pieces[offset][...].astype(bf16)
    acc[...] = jnp.zeros_like(acc)
    add_graph((sym, edges, degrees), shared, acc, me * share)
    add_data((users, items, count, factors, words), shared, acc)


def second_kernel(parts, count_sums, height, *refs):
    users, items, count, factors, words, sym, edges, degrees = refs[:8]
    pieces = refs[8 : 8 + parts]
    sums = refs[8 + parts : 8 + parts + count_sums]
    keep, send, scalars, own_z, own_w, shared, acc, start, image, move = refs[8 + parts + count_sums :]
    me, row = lax.axis_index("col"), lax.axis_index("row")
    share = pieces[0].shape[0]
    for offset in range(parts):
        block = (me ^ offset) * share
        start[pl.ds(block, share)] = pieces[offset][...]
    rhs = start[...]
    w = sum(ref[...].astype(f32) for ref in sums) + ridge_weight * rhs
    a, b = total(rhs * rhs), total(rhs * w)
    step = jnp.where(b > 0.0, a / jnp.where(b > 0.0, b, 1.0), 1.0)
    step = jnp.where(step > 0.0, step, 1.0)
    z = rhs - step * w
    image[...] = w
    move[...] = z
    high = z.astype(bf16)
    shared[:, : z.shape[1]] = high
    shared[:, z.shape[1] :] = (z - high.astype(f32)).astype(bf16)
    rz, zz, zw = total(rhs * z), total(z * z), total(z * w)
    acc[...] = jnp.zeros_like(acc)
    add_graph((sym, edges, degrees), shared, acc, me * share)
    add_data((users, items, count, factors, words), shared, acc)
    partial_value = acc[...]
    zh, rh = total(partial_value * move[...]), total(partial_value * start[...])
    part = 1.0 / parts
    values = (
        a * part,
        b * part,
        step,
        rz * part,
        zz * part,
        zw * part,
        zh + ridge_weight * part * zz,
        rh + ridge_weight * part * rz,
    )
    lane = lax.broadcasted_iota(jnp.int32, (height, 128), 1)
    sublane = lax.broadcasted_iota(jnp.int32, (height, 128), 0)
    packed = jnp.zeros((height, 128), f32)
    for index, value in enumerate(values):
        packed = jnp.where(lane == index, value, packed)
    scalars[...] = packed
    for j, mask in enumerate(even_masks(parts)):
        keep[pl.ds(j * share, share)] = acc[pl.ds((me ^ mask) * share, share)]
        send[pl.ds(j * share, share)] = acc[pl.ds((me ^ mask ^ 1) * share, share)]
    own_z[...] = move[pl.ds(me * share, share)]
    own_w[...] = image[pl.ds(me * share, share)]


def last_kernel(parts, scalar_parts, *refs):
    own_r, own_z, own_w = refs[:3]
    images = refs[3 : 3 + parts]
    scalars = refs[3 + parts : 3 + parts + scalar_parts]
    solution_ref, residual_ref = refs[3 + parts + scalar_parts :]
    table = scalars[0][...]
    for ref in scalars[1:]:
        table = table + ref[...]
    row = lax.axis_index("row")
    height = table.shape[0]
    a, b, step, rz, zz, zw, zh, rh = (table[:, k : k + 1] for k in range(8))

    def whole(value):
        return jnp.sum(value, axis=0, keepdims=True)

    norm = whole(a)
    alpha = norm / whole(b)
    rho = alpha / jnp.where(step > 0.0, step, 1.0)
    rest = 1.0 - rho
    norm_next = whole(rest * rest * a + 2.0 * rest * rho * rz + rho * rho * zz)
    beta = norm_next / norm
    p = rest + beta
    curve = whole(p * p * b + p * rho * (zw + rh) + rho * rho * zh)
    alpha_next = norm_next / curve
    sublane = lax.broadcasted_iota(jnp.int32, (height, 1), 0)
    mine = jnp.where(sublane == row * lax.axis_size("col"), rho, 0.0)
    rho = whole(mine)
    rest = 1.0 - rho
    p = rest + beta
    r, z, w = own_r[...], own_z[...], own_w[...]
    hz = ridge_weight * z
    for ref in images:
        hz = hz + ref[: z.shape[0]]
    solution_ref[...] = (alpha + alpha_next * p) * r + (alpha_next * rho) * z
    residual_ref[...] = rest * r + rho * z - alpha_next * (p * w + rho * hz)


def exchange(value, axes, size, offset):
    return lax.ppermute(value, axes, [(i, i ^ offset) for i in range(size)])


def bit_groups(size):
    bits = [1 << k for k in range(size.bit_length() - 1)]
    groups = [bits[:1]] + [bits[k : k + 2] for k in range(1, len(bits), 2)]
    return [group for group in groups if group]


def spans(group):
    offsets = [0]
    for bit in group:
        offsets = offsets + [offset ^ bit for offset in offsets]
    return offsets[1:]


def per_device(
    rows, cols, rhs, item_factors, slot_users, slot_items, slot_counts, mask_words, self_tiles, next_tiles
):
    share, rank, width = rhs.shape
    row_shape = (cols * share, rank, width)
    half = jax.ShapeDtypeStruct((cols * share // 2, rank, width), f32)
    piece = jax.ShapeDtypeStruct(rhs.shape, f32)
    params = pltpu.CompilerParams(vmem_limit_bytes=40 * 1024 * 1024)
    pieces = [rhs] + [exchange(rhs, "col", cols, offset) for offset in range(1, cols)]
    words = mask_words[0, 0]
    tile_shape = self_tiles.shape

    users, items = slot_users[0], slot_items[0]
    factors, words, users, items, sym, edges, degrees = pl.pallas_call(
        functools.partial(prepare_kernel, cols),
        out_shape=[
            jax.ShapeDtypeStruct(item_factors.shape, bf16),
            jax.ShapeDtypeStruct(words.shape, words.dtype),
            jax.ShapeDtypeStruct(users.shape, users.dtype),
            jax.ShapeDtypeStruct(items.shape, items.dtype),
            jax.ShapeDtypeStruct(tile_shape, bf16),
            jax.ShapeDtypeStruct(tile_shape, bf16),
            jax.ShapeDtypeStruct((tile_shape[0], 16, tile_shape[2]), f32),
        ],
        in_specs=[HBM] * 6,
        out_specs=[VMEM] * 7,
        scratch_shapes=[pltpu.VMEM((2,) + tile_shape, jnp.int32), pltpu.SemaphoreType.DMA((6,))],
        compiler_params=params,
        cost_estimate=pl.CostEstimate(flops=10**6, bytes_accessed=4 * 10**6, transcendentals=0),
        name="prepare",
    )(*(pltpu.with_memory_space_constraint(x, pltpu.HBM) for x in (item_factors, words, users, items, self_tiles, next_tiles)))
    cell = (users, items, slot_counts, factors, words, sym, edges, degrees)
    cell_specs = [SMEM] * 3 + [VMEM] * 5

    value = pl.pallas_call(
        functools.partial(first_kernel, cols),
        out_shape=jax.ShapeDtypeStruct(row_shape, f32),
        in_specs=cell_specs + [VMEM] * cols,
        out_specs=VMEM,
        scratch_shapes=[pltpu.VMEM(row_shape, bf16)],
        compiler_params=params,
        name="first_apply",
    )(*cell, *pieces)
    sums = [(value + exchange(value, "col", cols, 1)).astype(bf16)]
    for mask in even_masks(cols)[1:]:
        sums.append(exchange(sums[0], "col", cols, mask))

    height = rows * cols
    keep, send, table, own_z, own_w = pl.pallas_call(
        functools.partial(second_kernel, cols, len(sums), height),
        out_shape=[half, half, jax.ShapeDtypeStruct((height, 128), f32), piece, piece],
        in_specs=cell_specs + [VMEM] * (cols + len(sums)),
        out_specs=[VMEM] * 5,
        scratch_shapes=[pltpu.VMEM((cols * share, 2 * rank, width), bf16)] + [pltpu.VMEM(row_shape, f32)] * 4,
        compiler_params=params,
        name="second_apply",
    )(*cell, *pieces, *sums)
    pair = exchange(send, "col", cols, 1)
    images = [keep, pair]
    for j, mask in list(enumerate(even_masks(cols)))[1:]:
        block = slice(j * share, (j + 1) * share)
        images.append(exchange(keep[block] + pair[block], "col", cols, mask))
    tables = [lax.all_to_all(table, ("row", "col"), 0, 0, tiled=True)]

    return pl.pallas_call(
        functools.partial(last_kernel, len(images), len(tables)),
        out_shape=[piece, piece],
        in_specs=[VMEM] * (3 + len(images) + len(tables)),
        out_specs=[VMEM] * 2,
        compiler_params=params,
        name="last_update",
    )(rhs, own_z, own_w, *images, *tables)


def solution(mesh):
    rows, cols = mesh.shape["row"], mesh.shape["col"]
    return jax.shard_map(
        functools.partial(per_device, rows, cols),
        mesh=mesh,
        in_specs=(
            P(("row", "col"), None, None),
            P("col", None, None),
            P("row", "col", None),
            P("row", "col", None),
            P("row", "col"),
            P("row", "col", None, None, None),
            P(("row", "col"), None, None),
            P(("row", "col"), None, None),
        ),
        out_specs=(P(("row", "col"), None, None), P(("row", "col"), None, None)),
        check_vma=False,
    )
```

```python
import functools

import jax
import jax.numpy as jnp
from jax import lax
from jax.experimental import pallas as pl
from jax.experimental.pallas import tpu as pltpu
from jax.sharding import PartitionSpec as P

graph_weight = 0.01
ridge_weight = 0.5
unroll = 96
f32 = jnp.float32
bf16 = jnp.bfloat16

VMEM = pl.BlockSpec(memory_space=pltpu.VMEM)
HBM = pl.BlockSpec(memory_space=pltpu.HBM)
SMEM = pl.BlockSpec(memory_space=pltpu.SMEM)


def dot(a, b, dims):
    return lax.dot_general(a, b, ((dims[:1], dims[1:]), ((), ())), preferred_element_type=f32)


def add_data(cell, shared, acc):
    users, items, count_ref, factors, words = cell
    count = count_ref[0, 0]
    slots = users.shape[1]
    group = max(k for k in range(1, unroll + 1) if slots % k == 0)
    bit = jnp.left_shift(1, lax.broadcasted_iota(jnp.int32, (8, words.shape[2]), 0))

    def turn(index, carry):
        start = index * group
        for step in range(group):
            slot = start + step
            user, item = users[0, slot], items[0, slot]
            left = factors[item]
            pieces = shared.shape[1] // left.shape[0]
            scores = dot(jnp.concatenate([left] * pieces), shared[user], (0, 0))
            used = jnp.where(slot < count, bit, 0)
            mask = (words[slot][:, None, :] & used[None]) != 0
            tile = jnp.where(mask.reshape(scores.shape), scores, 0.0).astype(bf16)
            acc[user] += dot(left, tile, (1, 0))
        return carry

    if group == slots:
        turn(0, 0)
    else:
        lax.fori_loop(0, (count + group - 1) // group, turn, 0)


def add_graph(graph, shared, acc, first):
    sym, edges, degrees = graph
    row_blocks = shared.shape[0]
    for j in range(sym.shape[0]):
        local = first + j
        after = jnp.minimum(local + 1, row_blocks - 1)
        own, following = shared[local], shared[after]
        degree, column_degree = degrees[j, 0:1], degrees[j, 8:9]
        here = degree * own.astype(f32) - dot(own, sym[j], (1, 0)) - dot(following, edges[j], (1, 1))
        there = column_degree * following.astype(f32) - dot(own, edges[j], (1, 0))
        rank = acc.shape[1]
        here = sum(here[k : k + rank] for k in range(0, here.shape[0], rank))
        there = sum(there[k : k + rank] for k in range(0, there.shape[0], rank))
        acc[local] += graph_weight * here
        acc[after] += graph_weight * there


def prepare_kernel(cols, *refs):
    factors_in, words_in, users_in, items_in, self_in, next_in = refs[:6]
    factors, words, users, items, sym, edges, degrees, tiles, sems = refs[6:]
    first = lax.axis_index("col") * self_in.shape[0]
    copies = [
        pltpu.make_async_copy(source, target, sems.at[k])
        for k, (source, target) in enumerate(
            (
                (self_in, tiles.at[0]),
                (next_in, tiles.at[1]),
                (factors_in, factors),
                (words_in, words),
                (users_in, users),
                (items_in, items),
            )
        )
    ]
    for copy in copies:
        copy.start()
    copies[0].wait()
    copies[1].wait()
    count = self_in.shape[0]
    for j in range(count):
        keep = (first + j < cols * count - 1).astype(f32)
        weights = tiles[0, j].astype(f32)
        both = weights + weights.T
        edge = tiles[1, j].astype(f32) * keep
        edges_b = edge.astype(bf16)
        sym[j] = both.astype(bf16)
        edges[j] = edges_b
        ones = jnp.ones((8, both.shape[0]), bf16)
        degrees[j, 0:8] = jnp.sum(both, axis=0, keepdims=True) + dot(ones, edges_b, (1, 1))
        degrees[j, 8:16] = jnp.broadcast_to(jnp.sum(edge, axis=0, keepdims=True), (8, both.shape[1]))
    for copy in copies[2:]:
        copy.wait()


def even_masks(cols):
    return [mask for mask in range(cols) if bin(mask).count("1") % 2 == 0]


def total(value):
    return jnp.sum(jnp.sum(value, axis=tuple(range(value.ndim - 2))), keepdims=True)


def first_kernel(parts, *refs):
    users, items, count, factors, words, sym, edges, degrees = refs[:8]
    pieces = refs[8 : 8 + parts]
    acc, shared = refs[8 + parts :]
    me = lax.axis_index("col")
    share = pieces[0].shape[0]
    for offset in range(parts):
        block = (me ^ offset) * share
        shared[pl.ds(block, share)] = pieces[offset][...].astype(bf16)
    acc[...] = jnp.zeros_like(acc)
    add_graph((sym, edges, degrees), shared, acc, me * share)
    add_data((users, items, count, factors, words), shared, acc)


def second_kernel(parts, count_sums, height, *refs):
    users, items, count, factors, words, sym, edges, degrees = refs[:8]
    pieces = refs[8 : 8 + parts]
    sums = refs[8 + parts : 8 + parts + count_sums]
    keep, send, scalars, own_z, own_w, shared, acc, start, image, move = refs[8 + parts + count_sums :]
    me, row = lax.axis_index("col"), lax.axis_index("row")
    share = pieces[0].shape[0]
    for offset in range(parts):
        block = (me ^ offset) * share
        start[pl.ds(block, share)] = pieces[offset][...]
    rhs = start[...]
    w = sum(ref[...].astype(f32) for ref in sums) + ridge_weight * rhs
    a, b = total(rhs * rhs), total(rhs * w)
    step = jnp.where(b > 0.0, a / jnp.where(b > 0.0, b, 1.0), 1.0)
    step = jnp.where(step > 0.0, step, 1.0)
    z = rhs - step * w
    image[...] = w
    move[...] = z
    high = z.astype(bf16)
    shared[:, : z.shape[1]] = high
    shared[:, z.shape[1] :] = (z - high.astype(f32)).astype(bf16)
    rz, zz, zw = total(rhs * z), total(z * z), total(z * w)
    acc[...] = jnp.zeros_like(acc)
    add_graph((sym, edges, degrees), shared, acc, me * share)
    add_data((users, items, count, factors, words), shared, acc)
    partial_value = acc[...]
    zh, rh = total(partial_value * move[...]), total(partial_value * start[...])
    part = 1.0 / parts
    values = (
        a * part,
        b * part,
        step * part,
        rz * part,
        zz * part,
        zw * part,
        zh + ridge_weight * part * zz,
        rh + ridge_weight * part * rz,
    )
    lane = lax.broadcasted_iota(jnp.int32, (height, 128), 1)
    sublane = lax.broadcasted_iota(jnp.int32, (height, 128), 0)
    packed = jnp.zeros((height, 128), f32)
    for index, value in enumerate(values):
        packed = jnp.where(lane == index, value, packed)
    packed = jnp.where(sublane == row, packed, 0.0)
    scalars[...] = packed
    block = keep.shape[0] // (parts // 2)
    rank = block // share
    for j, mask in enumerate(even_masks(parts)):
        for i in range(share):
            rows = pl.ds(j * block + i * rank, rank)
            keep[rows] = acc[(me ^ mask) * share + i]
            send[rows] = acc[(me ^ mask ^ 1) * share + i]
    send[pl.ds(keep.shape[0], height)] = packed
    own_z[...] = move[pl.ds(me * share, share)]
    own_w[...] = image[pl.ds(me * share, share)]


def last_kernel(parts, scalar_parts, *refs):
    own_r, own_z, own_w = refs[:3]
    images = refs[3 : 3 + parts]
    scalars = refs[3 + parts : 3 + parts + scalar_parts]
    solution_ref, residual_ref = refs[3 + parts + scalar_parts :]
    table = scalars[0][...]
    for ref in scalars[1:]:
        table = table + ref[...]
    row = lax.axis_index("row")
    height = table.shape[0]
    a, b, step, rz, zz, zw, zh, rh = (table[:, k : k + 1] for k in range(8))

    def whole(value):
        return jnp.sum(value, axis=0, keepdims=True)

    norm = whole(a)
    alpha = norm / whole(b)
    rho = alpha / jnp.where(step > 0.0, step, 1.0)
    rest = 1.0 - rho
    norm_next = whole(rest * rest * a + 2.0 * rest * rho * rz + rho * rho * zz)
    beta = norm_next / norm
    p = rest + beta
    curve = whole(p * p * b + p * rho * (zw + rh) + rho * rho * zh)
    alpha_next = norm_next / curve
    sublane = lax.broadcasted_iota(jnp.int32, (height, 1), 0)
    mine = jnp.where(sublane == row, rho, 0.0)
    rho = whole(mine)
    rest = 1.0 - rho
    p = rest + beta
    r, z, w = own_r[...], own_z[...], own_w[...]
    hz = ridge_weight * z
    for ref in images:
        hz = hz + ref[: z.shape[0] * z.shape[1]].reshape(z.shape)
    solution_ref[...] = (alpha + alpha_next * p) * r + (alpha_next * rho) * z
    residual_ref[...] = rest * r + rho * z - alpha_next * (p * w + rho * hz)


def exchange(value, axes, size, offset):
    return lax.ppermute(value, axes, [(i, i ^ offset) for i in range(size)])


def stages(rows, cols):
    first = even_masks(cols)[1:]
    if rows > 1:
        first = first + [(mask ^ cols) | 1 for mask in even_masks(cols)]
    bits = [cols << k for k in range(1, rows.bit_length() - 1)]
    return [first] + [[bit | 1] for bit in bits]


def per_device(
    rows, cols, rhs, item_factors, slot_users, slot_items, slot_counts, mask_words, self_tiles, next_tiles
):
    share, rank, width = rhs.shape
    row_shape = (cols * share, rank, width)
    half = jax.ShapeDtypeStruct((cols * share // 2, rank, width), f32)
    piece = jax.ShapeDtypeStruct(rhs.shape, f32)
    params = pltpu.CompilerParams(vmem_limit_bytes=40 * 1024 * 1024)
    pieces = [rhs] + [exchange(rhs, "col", cols, offset) for offset in range(1, cols)]
    words = mask_words[0, 0]
    tile_shape = self_tiles.shape

    users, items = slot_users[0], slot_items[0]
    factors, words, users, items, sym, edges, degrees = pl.pallas_call(
        functools.partial(prepare_kernel, cols),
        out_shape=[
            jax.ShapeDtypeStruct(item_factors.shape, bf16),
            jax.ShapeDtypeStruct(words.shape, words.dtype),
            pltpu.SMEM(users.shape, users.dtype),
            pltpu.SMEM(items.shape, items.dtype),
            jax.ShapeDtypeStruct(tile_shape, bf16),
            jax.ShapeDtypeStruct(tile_shape, bf16),
            jax.ShapeDtypeStruct((tile_shape[0], 16, tile_shape[2]), f32),
        ],
        in_specs=[HBM] * 6,
        out_specs=[VMEM] * 2 + [SMEM] * 2 + [VMEM] * 3,
        scratch_shapes=[pltpu.VMEM((2,) + tile_shape, jnp.int32), pltpu.SemaphoreType.DMA((6,))],
        compiler_params=params,
        cost_estimate=pl.CostEstimate(flops=10**6, bytes_accessed=4 * 10**6, transcendentals=0),
        name="prepare",
    )(*(pltpu.with_memory_space_constraint(x, pltpu.HBM) for x in (item_factors, words, users, items, self_tiles, next_tiles)))
    cell = (users, items, slot_counts, factors, words, sym, edges, degrees)
    cell_specs = [SMEM] * 3 + [VMEM] * 5

    value = pl.pallas_call(
        functools.partial(first_kernel, cols),
        out_shape=jax.ShapeDtypeStruct(row_shape, f32),
        in_specs=cell_specs + [VMEM] * cols,
        out_specs=VMEM,
        scratch_shapes=[pltpu.VMEM(row_shape, bf16)],
        compiler_params=params,
        name="first_apply",
    )(*cell, *pieces)
    sums = [(value + exchange(value, "col", cols, 1)).astype(bf16)]
    for mask in even_masks(cols)[1:]:
        sums.append(exchange(sums[0], "col", cols, mask))

    height = -(-rows // 8) * 8
    block = share * rank
    flat = jax.ShapeDtypeStruct((cols // 2 * block, width), f32)
    tall = jax.ShapeDtypeStruct((cols // 2 * block + height, width), f32)
    keep, send, table, own_z, own_w = pl.pallas_call(
        functools.partial(second_kernel, cols, len(sums), height),
        out_shape=[flat, tall, jax.ShapeDtypeStruct((height, 128), f32), piece, piece],
        in_specs=cell_specs + [VMEM] * (cols + len(sums)),
        out_specs=[VMEM] * 5,
        scratch_shapes=[pltpu.VMEM((cols * share, 2 * rank, width), bf16)] + [pltpu.VMEM(row_shape, f32)] * 4,
        compiler_params=params,
        name="second_apply",
    )(*cell, *pieces, *sums)
    pair = exchange(send, "col", cols, 1)
    tables = [table, pair[-height:]]
    images = [keep, pair]
    for group in stages(rows, cols):
        table = functools.reduce(jnp.add, tables)
        tables = [table]
        for mask in group:
            if mask < cols:
                j = even_masks(cols).index(mask)
                part = slice(j * block, (j + 1) * block)
                images.append(exchange(jnp.concatenate([keep[part] + pair[part], table]), "col", cols, mask))
                tables.append(images[-1][-height:])
            else:
                tables.append(exchange(table, ("row", "col"), rows * cols, mask))

    return pl.pallas_call(
        functools.partial(last_kernel, len(images), len(tables)),
        out_shape=[piece, piece],
        in_specs=[VMEM] * (3 + len(images) + len(tables)),
        out_specs=[VMEM] * 2,
        compiler_params=params,
        name="last_update",
    )(rhs, own_z, own_w, *images, *tables)


def solution(mesh):
    rows, cols = mesh.shape["row"], mesh.shape["col"]
    return jax.shard_map(
        functools.partial(per_device, rows, cols),
        mesh=mesh,
        in_specs=(
            P(("row", "col"), None, None),
            P("col", None, None),
            P("row", "col", None),
            P("row", "col", None),
            P("row", "col"),
            P("row", "col", None, None, None),
            P(("row", "col"), None, None),
            P(("row", "col"), None, None),
        ),
        out_specs=(P(("row", "col"), None, None), P(("row", "col"), None, None)),
        check_vma=False,
    )
```

```python
import functools

import jax
import jax.numpy as jnp
from jax import lax
from jax.experimental import pallas as pl
from jax.experimental.pallas import tpu as pltpu
from jax.sharding import PartitionSpec as P

graph_weight = 0.01
ridge_weight = 0.5
unroll = 96
f32 = jnp.float32
bf16 = jnp.bfloat16

VMEM = pl.BlockSpec(memory_space=pltpu.VMEM)
HBM = pl.BlockSpec(memory_space=pltpu.HBM)
SMEM = pl.BlockSpec(memory_space=pltpu.SMEM)


def dot(a, b, dims):
    return lax.dot_general(a, b, ((dims[:1], dims[1:]), ((), ())), preferred_element_type=f32)


def add_data(cell, shared, acc):
    users, items, count_ref, factors, words = cell
    count = count_ref[0, 0]
    slots = users.shape[1]
    group = max(k for k in range(1, unroll + 1) if slots % k == 0)
    bit = jnp.left_shift(1, lax.broadcasted_iota(jnp.int32, (8, words.shape[2]), 0))

    def turn(index, carry):
        start = index * group
        for step in range(group):
            slot = start + step
            user, item = users[0, slot], items[0, slot]
            left = factors[item]
            pieces = shared.shape[1] // left.shape[0]
            scores = dot(jnp.concatenate([left] * pieces), shared[user], (0, 0))
            used = jnp.where(slot < count, bit, 0)
            mask = (words[slot][:, None, :] & used[None]) != 0
            tile = jnp.where(mask.reshape(scores.shape), scores, 0.0).astype(bf16)
            acc[user] += dot(left, tile, (1, 0))
        return carry

    if group == slots:
        turn(0, 0)
    else:
        lax.fori_loop(0, (count + group - 1) // group, turn, 0)


def add_graph(graph, shared, acc, first):
    sym, edges, degrees = graph
    row_blocks = shared.shape[0]
    for j in range(sym.shape[0]):
        local = first + j
        after = jnp.minimum(local + 1, row_blocks - 1)
        own, following = shared[local], shared[after]
        degree, column_degree = degrees[j, 0:1], degrees[j, 8:9]
        here = degree * own.astype(f32) - dot(own, sym[j], (1, 0)) - dot(following, edges[j], (1, 1))
        there = column_degree * following.astype(f32) - dot(own, edges[j], (1, 0))
        rank = acc.shape[1]
        here = sum(here[k : k + rank] for k in range(0, here.shape[0], rank))
        there = sum(there[k : k + rank] for k in range(0, there.shape[0], rank))
        acc[local] += graph_weight * here
        acc[after] += graph_weight * there


def prepare_kernel(cols, *refs):
    factors_in, words_in, users_in, items_in, self_in, next_in = refs[:6]
    factors, words, users, items, sym, edges, degrees, tiles, sems = refs[6:]
    first = lax.axis_index("col") * self_in.shape[0]
    copies = [
        pltpu.make_async_copy(source, target, sems.at[k])
        for k, (source, target) in enumerate(
            (
                (self_in, tiles.at[0]),
                (next_in, tiles.at[1]),
                (factors_in, factors),
                (words_in, words),
                (users_in, users),
                (items_in, items),
            )
        )
    ]
    for copy in copies:
        copy.start()
    copies[0].wait()
    copies[1].wait()
    count = self_in.shape[0]
    for j in range(count):
        keep = (first + j < cols * count - 1).astype(f32)
        weights = tiles[0, j].astype(f32)
        both = weights + weights.T
        edge = tiles[1, j].astype(f32) * keep
        edges_b = edge.astype(bf16)
        sym[j] = both.astype(bf16)
        edges[j] = edges_b
        ones = jnp.ones((8, both.shape[0]), bf16)
        degrees[j, 0:8] = jnp.sum(both, axis=0, keepdims=True) + dot(ones, edges_b, (1, 1))
        degrees[j, 8:16] = jnp.broadcast_to(jnp.sum(edge, axis=0, keepdims=True), (8, both.shape[1]))
    for copy in copies[2:]:
        copy.wait()


def even_masks(cols):
    return [mask for mask in range(cols) if bin(mask).count("1") % 2 == 0]


def total(value):
    return jnp.sum(jnp.sum(value, axis=tuple(range(value.ndim - 2))), keepdims=True)


def first_kernel(parts, *refs):
    users, items, count, factors, words, sym, edges, degrees = refs[:8]
    pieces = refs[8 : 8 + parts]
    acc, start, shared = refs[8 + parts :]
    me = lax.axis_index("col")
    share = pieces[0].shape[0]
    for offset in range(parts):
        block = (me ^ offset) * share
        piece = pieces[offset][...]
        start[pl.ds(block, share)] = piece
        shared[pl.ds(block, share)] = piece.astype(bf16)
    acc[...] = jnp.zeros_like(acc)
    add_graph((sym, edges, degrees), shared, acc, me * share)
    add_data((users, items, count, factors, words), shared, acc)


def second_kernel(parts, count_sums, height, *refs):
    users, items, count, factors, words, sym, edges, degrees = refs[:8]
    start = refs[8]
    sums = refs[9 : 9 + count_sums]
    keep, send, scalars, own_z, own_w, shared, acc, image, move = refs[9 + count_sums :]
    me, row = lax.axis_index("col"), lax.axis_index("row")
    share = start.shape[0] // parts
    rhs = start[...]
    w = sum(ref[...].astype(f32) for ref in sums) + ridge_weight * rhs
    a, b = total(rhs * rhs), total(rhs * w)
    step = jnp.where(b > 0.0, a / jnp.where(b > 0.0, b, 1.0), 1.0)
    step = jnp.where(step > 0.0, step, 1.0)
    z = rhs - step * w
    image[...] = w
    move[...] = z
    high = z.astype(bf16)
    shared[:, : z.shape[1]] = high
    shared[:, z.shape[1] :] = (z - high.astype(f32)).astype(bf16)
    rz, zz, zw = total(rhs * z), total(z * z), total(z * w)
    acc[...] = jnp.zeros_like(acc)
    add_graph((sym, edges, degrees), shared, acc, me * share)
    add_data((users, items, count, factors, words), shared, acc)
    partial_value = acc[...]
    zh, rh = total(partial_value * move[...]), total(partial_value * start[...])
    part = 1.0 / parts
    values = (
        a * part,
        b * part,
        step * part,
        rz * part,
        zz * part,
        zw * part,
        zh + ridge_weight * part * zz,
        rh + ridge_weight * part * rz,
    )
    lane = lax.broadcasted_iota(jnp.int32, (height, 128), 1)
    sublane = lax.broadcasted_iota(jnp.int32, (height, 128), 0)
    packed = jnp.zeros((height, 128), f32)
    for index, value in enumerate(values):
        packed = jnp.where(lane == index, value, packed)
    packed = jnp.where(sublane == row, packed, 0.0)
    scalars[...] = packed
    block = keep.shape[0] // (parts // 2)
    rank = block // share
    for j, mask in enumerate(even_masks(parts)):
        for i in range(share):
            rows = pl.ds(j * block + i * rank, rank)
            keep[rows] = acc[(me ^ mask) * share + i]
            send[rows] = acc[(me ^ mask ^ 1) * share + i]
    send[pl.ds(keep.shape[0], height)] = packed
    own_z[...] = move[pl.ds(me * share, share)]
    own_w[...] = image[pl.ds(me * share, share)]


def last_kernel(parts, scalar_parts, *refs):
    own_r, own_z, own_w = refs[:3]
    images = refs[3 : 3 + parts]
    scalars = refs[3 + parts : 3 + parts + scalar_parts]
    solution_ref, residual_ref = refs[3 + parts + scalar_parts :]
    table = scalars[0][...]
    for ref in scalars[1:]:
        table = table + ref[...]
    row = lax.axis_index("row")
    height = table.shape[0]
    a, b, step, rz, zz, zw, zh, rh = (table[:, k : k + 1] for k in range(8))

    def whole(value):
        return jnp.sum(value, axis=0, keepdims=True)

    norm = whole(a)
    alpha = norm / whole(b)
    rho = alpha / jnp.where(step > 0.0, step, 1.0)
    rest = 1.0 - rho
    norm_next = whole(rest * rest * a + 2.0 * rest * rho * rz + rho * rho * zz)
    beta = norm_next / norm
    p = rest + beta
    curve = whole(p * p * b + p * rho * (zw + rh) + rho * rho * zh)
    alpha_next = norm_next / curve
    sublane = lax.broadcasted_iota(jnp.int32, (height, 1), 0)
    mine = jnp.where(sublane == row, rho, 0.0)
    rho = whole(mine)
    rest = 1.0 - rho
    p = rest + beta
    r, z, w = own_r[...], own_z[...], own_w[...]
    hz = ridge_weight * z
    for ref in images:
        hz = hz + ref[: z.shape[0] * z.shape[1]].reshape(z.shape)
    solution_ref[...] = (alpha + alpha_next * p) * r + (alpha_next * rho) * z
    residual_ref[...] = rest * r + rho * z - alpha_next * (p * w + rho * hz)


def exchange(value, axes, size, offset):
    return lax.ppermute(value, axes, [(i, i ^ offset) for i in range(size)])


def stages(rows, cols):
    first = even_masks(cols)[1:]
    if rows > 1:
        first = first + [(mask ^ cols) | 1 for mask in even_masks(cols)]
    bits = [cols << k for k in range(1, rows.bit_length() - 1)]
    return [first] + [[bit | 1] for bit in bits]


def per_device(
    rows, cols, rhs, item_factors, slot_users, slot_items, slot_counts, mask_words, self_tiles, next_tiles
):
    share, rank, width = rhs.shape
    row_shape = (cols * share, rank, width)
    half = jax.ShapeDtypeStruct((cols * share // 2, rank, width), f32)
    piece = jax.ShapeDtypeStruct(rhs.shape, f32)
    params = pltpu.CompilerParams(vmem_limit_bytes=40 * 1024 * 1024)
    pieces = [rhs] + [exchange(rhs, "col", cols, offset) for offset in range(1, cols)]
    words = mask_words[0, 0]
    tile_shape = self_tiles.shape

    users, items = slot_users[0], slot_items[0]
    factors, words, users, items, sym, edges, degrees = pl.pallas_call(
        functools.partial(prepare_kernel, cols),
        out_shape=[
            jax.ShapeDtypeStruct(item_factors.shape, bf16),
            jax.ShapeDtypeStruct(words.shape, words.dtype),
            pltpu.SMEM(users.shape, users.dtype),
            pltpu.SMEM(items.shape, items.dtype),
            jax.ShapeDtypeStruct(tile_shape, bf16),
            jax.ShapeDtypeStruct(tile_shape, bf16),
            jax.ShapeDtypeStruct((tile_shape[0], 16, tile_shape[2]), f32),
        ],
        in_specs=[HBM] * 6,
        out_specs=[VMEM] * 2 + [SMEM] * 2 + [VMEM] * 3,
        scratch_shapes=[pltpu.VMEM((2,) + tile_shape, jnp.int32), pltpu.SemaphoreType.DMA((6,))],
        compiler_params=params,
        cost_estimate=pl.CostEstimate(flops=10**6, bytes_accessed=4 * 10**6, transcendentals=0),
        name="prepare",
    )(*(pltpu.with_memory_space_constraint(x, pltpu.HBM) for x in (item_factors, words, users, items, self_tiles, next_tiles)))
    cell = (users, items, slot_counts, factors, words, sym, edges, degrees)
    cell_specs = [SMEM] * 3 + [VMEM] * 5

    whole = jax.ShapeDtypeStruct(row_shape, f32)
    value, start = pl.pallas_call(
        functools.partial(first_kernel, cols),
        out_shape=[whole, whole],
        in_specs=cell_specs + [VMEM] * cols,
        out_specs=[VMEM] * 2,
        scratch_shapes=[pltpu.VMEM(row_shape, bf16)],
        compiler_params=params,
        name="first_apply",
    )(*cell, *pieces)
    sums = [(value + exchange(value, "col", cols, 1)).astype(bf16)]
    for mask in even_masks(cols)[1:]:
        sums.append(exchange(sums[0], "col", cols, mask))

    height = -(-rows // 8) * 8
    block = share * rank
    flat = jax.ShapeDtypeStruct((cols // 2 * block, width), f32)
    tall = jax.ShapeDtypeStruct((cols // 2 * block + height, width), f32)
    keep, send, table, own_z, own_w = pl.pallas_call(
        functools.partial(second_kernel, cols, len(sums), height),
        out_shape=[flat, tall, jax.ShapeDtypeStruct((height, 128), f32), piece, piece],
        in_specs=cell_specs + [VMEM] * (1 + len(sums)),
        out_specs=[VMEM] * 5,
        scratch_shapes=[pltpu.VMEM((cols * share, 2 * rank, width), bf16)] + [pltpu.VMEM(row_shape, f32)] * 3,
        compiler_params=params,
        name="second_apply",
    )(*cell, start, *sums)
    pair = exchange(send, "col", cols, 1)
    tables = [table, pair[-height:]]
    images = [keep, pair]
    for group in stages(rows, cols):
        table = functools.reduce(jnp.add, tables)
        tables = [table]
        for mask in group:
            if mask < cols:
                j = even_masks(cols).index(mask)
                part = slice(j * block, (j + 1) * block)
                images.append(exchange(jnp.concatenate([keep[part] + pair[part], table]), "col", cols, mask))
                tables.append(images[-1][-height:])
            else:
                tables.append(exchange(table, ("row", "col"), rows * cols, mask))

    return pl.pallas_call(
        functools.partial(last_kernel, len(images), len(tables)),
        out_shape=[piece, piece],
        in_specs=[VMEM] * (3 + len(images) + len(tables)),
        out_specs=[VMEM] * 2,
        compiler_params=params,
        name="last_update",
    )(rhs, own_z, own_w, *images, *tables)


def solution(mesh):
    rows, cols = mesh.shape["row"], mesh.shape["col"]
    return jax.shard_map(
        functools.partial(per_device, rows, cols),
        mesh=mesh,
        in_specs=(
            P(("row", "col"), None, None),
            P("col", None, None),
            P("row", "col", None),
            P("row", "col", None),
            P("row", "col"),
            P("row", "col", None, None, None),
            P(("row", "col"), None, None),
            P(("row", "col"), None, None),
        ),
        out_specs=(P(("row", "col"), None, None), P(("row", "col"), None, None)),
        check_vma=False,
    )
```

```python
import functools

import jax
import jax.numpy as jnp
from jax import lax
from jax.experimental import pallas as pl
from jax.experimental.pallas import tpu as pltpu
from jax.sharding import PartitionSpec as P

graph_weight = 0.01
ridge_weight = 0.5
unroll = 96
f32 = jnp.float32
bf16 = jnp.bfloat16

VMEM = pl.BlockSpec(memory_space=pltpu.VMEM)
HBM = pl.BlockSpec(memory_space=pltpu.HBM)
SMEM = pl.BlockSpec(memory_space=pltpu.SMEM)


def dot(a, b, dims):
    return lax.dot_general(a, b, ((dims[:1], dims[1:]), ((), ())), preferred_element_type=f32)


def add_data(cell, shared, acc):
    users, items, count_ref, factors, words = cell
    count = count_ref[0, 0]
    slots = users.shape[1]
    group = max(k for k in range(1, unroll + 1) if slots % k == 0)
    bit = jnp.left_shift(1, lax.broadcasted_iota(jnp.int32, (8, words.shape[2]), 0))

    def turn(index, carry):
        start = index * group
        for step in range(group):
            slot = start + step
            user, item = users[0, slot], items[0, slot]
            left = factors[item]
            pieces = shared.shape[1] // left.shape[0]
            scores = dot(jnp.concatenate([left] * pieces), shared[user], (0, 0))
            used = jnp.where(slot < count, bit, 0)
            mask = (words[slot][:, None, :] & used[None]) != 0
            tile = jnp.where(mask.reshape(scores.shape), scores, 0.0).astype(bf16)
            acc[user] += dot(left, tile, (1, 0))
        return carry

    if group == slots:
        turn(0, 0)
    else:
        lax.fori_loop(0, (count + group - 1) // group, turn, 0)


def add_graph(graph, shared, acc, first):
    sym, edges, degrees = graph
    row_blocks = shared.shape[0]
    for j in range(sym.shape[0]):
        local = first + j
        after = jnp.minimum(local + 1, row_blocks - 1)
        own, following = shared[local], shared[after]
        degree, column_degree = degrees[j, 0:1], degrees[j, 8:9]
        here = degree * own.astype(f32) - dot(own, sym[j], (1, 0)) - dot(following, edges[j], (1, 1))
        there = column_degree * following.astype(f32) - dot(own, edges[j], (1, 0))
        rank = acc.shape[1]
        here = sum(here[k : k + rank] for k in range(0, here.shape[0], rank))
        there = sum(there[k : k + rank] for k in range(0, there.shape[0], rank))
        acc[local] += graph_weight * here
        acc[after] += graph_weight * there


def prepare_kernel(cols, *refs):
    factors_in, words_in, users_in, items_in, self_in, next_in = refs[:6]
    factors, words, users, items, sym, edges, degrees, tiles, sems = refs[6:]
    first = lax.axis_index("col") * self_in.shape[0]
    copies = [
        pltpu.make_async_copy(source, target, sems.at[k])
        for k, (source, target) in enumerate(
            (
                (self_in, tiles.at[0]),
                (next_in, tiles.at[1]),
                (factors_in, factors),
                (words_in, words),
                (users_in, users),
                (items_in, items),
            )
        )
    ]
    for copy in copies:
        copy.start()
    copies[0].wait()
    copies[1].wait()
    count = self_in.shape[0]
    for j in range(count):
        keep = (first + j < cols * count - 1).astype(f32)
        weights = tiles[0, j].astype(f32)
        both = weights + weights.T
        edge = tiles[1, j].astype(f32) * keep
        edges_b = edge.astype(bf16)
        sym[j] = both.astype(bf16)
        edges[j] = edges_b
        ones = jnp.ones((8, both.shape[0]), bf16)
        degrees[j, 0:8] = jnp.sum(both, axis=0, keepdims=True) + dot(ones, edges_b, (1, 1))
        degrees[j, 8:16] = jnp.broadcast_to(jnp.sum(edge, axis=0, keepdims=True), (8, both.shape[1]))
    for copy in copies[2:]:
        copy.wait()


def even_masks(cols):
    return [mask for mask in range(cols) if bin(mask).count("1") % 2 == 0]


def total(value):
    return jnp.sum(jnp.sum(value, axis=tuple(range(value.ndim - 2))), keepdims=True)


def first_kernel(parts, *refs):
    users, items, count, factors, words, sym, edges, degrees = refs[:8]
    pieces = refs[8 : 8 + parts]
    value, start, shared, acc = refs[8 + parts :]
    me = lax.axis_index("col")
    share = pieces[0].shape[0]
    for offset in range(parts):
        block = (me ^ offset) * share
        piece = pieces[offset][...]
        start[pl.ds(block, share)] = piece
        shared[pl.ds(block, share)] = piece.astype(bf16)
    acc[...] = jnp.zeros_like(acc)
    add_graph((sym, edges, degrees), shared, acc, me * share)
    add_data((users, items, count, factors, words), shared, acc)
    value[...] = acc[...].astype(bf16)


def second_kernel(parts, count_sums, height, *refs):
    users, items, count, factors, words, sym, edges, degrees = refs[:8]
    start = refs[8]
    sums = refs[9 : 9 + count_sums]
    keep, send, scalars, own_z, own_w, shared, acc, image, move = refs[9 + count_sums :]
    me, row = lax.axis_index("col"), lax.axis_index("row")
    share = start.shape[0] // parts
    rhs = start[...]
    pairs = [near[...].astype(f32) + far[...].astype(f32) for near, far in zip(sums[::2], sums[1::2])]
    w = sum(pairs) + ridge_weight * rhs
    a, b = total(rhs * rhs), total(rhs * w)
    step = jnp.where(b > 0.0, a / jnp.where(b > 0.0, b, 1.0), 1.0)
    step = jnp.where(step > 0.0, step, 1.0)
    z = rhs - step * w
    image[...] = w
    move[...] = z
    high = z.astype(bf16)
    shared[:, : z.shape[1]] = high
    shared[:, z.shape[1] :] = (z - high.astype(f32)).astype(bf16)
    rz, zz, zw = total(rhs * z), total(z * z), total(z * w)
    acc[...] = jnp.zeros_like(acc)
    add_graph((sym, edges, degrees), shared, acc, me * share)
    add_data((users, items, count, factors, words), shared, acc)
    partial_value = acc[...]
    zh, rh = total(partial_value * move[...]), total(partial_value * start[...])
    part = 1.0 / parts
    values = (
        a * part,
        b * part,
        step * part,
        rz * part,
        zz * part,
        zw * part,
        zh + ridge_weight * part * zz,
        rh + ridge_weight * part * rz,
    )
    lane = lax.broadcasted_iota(jnp.int32, (height, 128), 1)
    sublane = lax.broadcasted_iota(jnp.int32, (height, 128), 0)
    packed = jnp.zeros((height, 128), f32)
    for index, value in enumerate(values):
        packed = jnp.where(lane == index, value, packed)
    packed = jnp.where(sublane == row, packed, 0.0)
    scalars[...] = packed
    block = keep.shape[0] // (parts // 2)
    rank = block // share
    for j, mask in enumerate(even_masks(parts)):
        for i in range(share):
            rows = pl.ds(j * block + i * rank, rank)
            keep[rows] = acc[(me ^ mask) * share + i]
            send[rows] = acc[(me ^ mask ^ 1) * share + i]
    send[pl.ds(keep.shape[0], height)] = packed
    own_z[...] = move[pl.ds(me * share, share)]
    own_w[...] = image[pl.ds(me * share, share)]


def last_kernel(parts, scalar_parts, *refs):
    own_r, own_z, own_w = refs[:3]
    images = refs[3 : 3 + parts]
    scalars = refs[3 + parts : 3 + parts + scalar_parts]
    solution_ref, residual_ref = refs[3 + parts + scalar_parts :]
    table = scalars[0][...]
    for ref in scalars[1:]:
        table = table + ref[...]
    row = lax.axis_index("row")
    height = table.shape[0]
    a, b, step, rz, zz, zw, zh, rh = (table[:, k : k + 1] for k in range(8))

    def whole(value):
        return jnp.sum(value, axis=0, keepdims=True)

    norm = whole(a)
    alpha = norm / whole(b)
    rho = alpha / jnp.where(step > 0.0, step, 1.0)
    rest = 1.0 - rho
    norm_next = whole(rest * rest * a + 2.0 * rest * rho * rz + rho * rho * zz)
    beta = norm_next / norm
    p = rest + beta
    curve = whole(p * p * b + p * rho * (zw + rh) + rho * rho * zh)
    alpha_next = norm_next / curve
    sublane = lax.broadcasted_iota(jnp.int32, (height, 1), 0)
    mine = jnp.where(sublane == row, rho, 0.0)
    rho = whole(mine)
    rest = 1.0 - rho
    p = rest + beta
    r, z, w = own_r[...], own_z[...], own_w[...]
    hz = ridge_weight * z
    for ref in images:
        hz = hz + ref[: z.shape[0] * z.shape[1]].reshape(z.shape)
    solution_ref[...] = (alpha + alpha_next * p) * r + (alpha_next * rho) * z
    residual_ref[...] = rest * r + rho * z - alpha_next * (p * w + rho * hz)


def exchange(value, axes, size, offset):
    return lax.ppermute(value, axes, [(i, i ^ offset) for i in range(size)])


def stages(rows, cols):
    first = even_masks(cols)[1:]
    if rows > 1:
        first = first + [(mask ^ cols) | 1 for mask in even_masks(cols)]
    bits = [cols << k for k in range(1, rows.bit_length() - 1)]
    return [first] + [[bit | 1] for bit in bits]


def per_device(
    rows, cols, rhs, item_factors, slot_users, slot_items, slot_counts, mask_words, self_tiles, next_tiles
):
    share, rank, width = rhs.shape
    row_shape = (cols * share, rank, width)
    half = jax.ShapeDtypeStruct((cols * share // 2, rank, width), f32)
    piece = jax.ShapeDtypeStruct(rhs.shape, f32)
    params = pltpu.CompilerParams(vmem_limit_bytes=40 * 1024 * 1024)
    pieces = [rhs] + [exchange(rhs, "col", cols, offset) for offset in range(1, cols)]
    words = mask_words[0, 0]
    tile_shape = self_tiles.shape

    users, items = slot_users[0], slot_items[0]
    factors, words, users, items, sym, edges, degrees = pl.pallas_call(
        functools.partial(prepare_kernel, cols),
        out_shape=[
            jax.ShapeDtypeStruct(item_factors.shape, bf16),
            jax.ShapeDtypeStruct(words.shape, words.dtype),
            pltpu.SMEM(users.shape, users.dtype),
            pltpu.SMEM(items.shape, items.dtype),
            jax.ShapeDtypeStruct(tile_shape, bf16),
            jax.ShapeDtypeStruct(tile_shape, bf16),
            jax.ShapeDtypeStruct((tile_shape[0], 16, tile_shape[2]), f32),
        ],
        in_specs=[HBM] * 6,
        out_specs=[VMEM] * 2 + [SMEM] * 2 + [VMEM] * 3,
        scratch_shapes=[pltpu.VMEM((2,) + tile_shape, jnp.int32), pltpu.SemaphoreType.DMA((6,))],
        compiler_params=params,
        cost_estimate=pl.CostEstimate(flops=10**6, bytes_accessed=4 * 10**6, transcendentals=0),
        name="prepare",
    )(*(pltpu.with_memory_space_constraint(x, pltpu.HBM) for x in (item_factors, words, users, items, self_tiles, next_tiles)))
    cell = (users, items, slot_counts, factors, words, sym, edges, degrees)
    cell_specs = [SMEM] * 3 + [VMEM] * 5

    whole = jax.ShapeDtypeStruct(row_shape, f32)
    value, start = pl.pallas_call(
        functools.partial(first_kernel, cols),
        out_shape=[jax.ShapeDtypeStruct(row_shape, bf16), whole],
        in_specs=cell_specs + [VMEM] * cols,
        out_specs=[VMEM] * 2,
        scratch_shapes=[pltpu.VMEM(row_shape, bf16), pltpu.VMEM(row_shape, f32)],
        compiler_params=params,
        name="first_apply",
    )(*cell, *pieces)
    sums = []
    for mask in even_masks(cols):
        near = exchange(value, "col", cols, mask) if mask else value
        sums += [near, exchange(near, "col", cols, 1)]

    height = -(-rows // 8) * 8
    block = share * rank
    flat = jax.ShapeDtypeStruct((cols // 2 * block, width), f32)
    tall = jax.ShapeDtypeStruct((cols // 2 * block + height, width), f32)
    keep, send, table, own_z, own_w = pl.pallas_call(
        functools.partial(second_kernel, cols, len(sums), height),
        out_shape=[flat, tall, jax.ShapeDtypeStruct((height, 128), f32), piece, piece],
        in_specs=cell_specs + [VMEM] * (1 + len(sums)),
        out_specs=[VMEM] * 5,
        scratch_shapes=[pltpu.VMEM((cols * share, 2 * rank, width), bf16)] + [pltpu.VMEM(row_shape, f32)] * 3,
        compiler_params=params,
        name="second_apply",
    )(*cell, start, *sums)
    pair = exchange(send, "col", cols, 1)
    tables = [table, pair[-height:]]
    images = [keep, pair]
    for group in stages(rows, cols):
        table = functools.reduce(jnp.add, tables)
        tables = [table]
        for mask in group:
            if mask < cols:
                j = even_masks(cols).index(mask)
                part = slice(j * block, (j + 1) * block)
                images.append(exchange(jnp.concatenate([keep[part] + pair[part], table]), "col", cols, mask))
                tables.append(images[-1][-height:])
            else:
                tables.append(exchange(table, ("row", "col"), rows * cols, mask))

    return pl.pallas_call(
        functools.partial(last_kernel, len(images), len(tables)),
        out_shape=[piece, piece],
        in_specs=[VMEM] * (3 + len(images) + len(tables)),
        out_specs=[VMEM] * 2,
        compiler_params=params,
        name="last_update",
    )(rhs, own_z, own_w, *images, *tables)


def solution(mesh):
    rows, cols = mesh.shape["row"], mesh.shape["col"]
    return jax.shard_map(
        functools.partial(per_device, rows, cols),
        mesh=mesh,
        in_specs=(
            P(("row", "col"), None, None),
            P("col", None, None),
            P("row", "col", None),
            P("row", "col", None),
            P("row", "col"),
            P("row", "col", None, None, None),
            P(("row", "col"), None, None),
            P(("row", "col"), None, None),
        ),
        out_specs=(P(("row", "col"), None, None), P(("row", "col"), None, None)),
        check_vma=False,
    )
```
